32 devices in a mesh: grp: 2 (over x), ep: 16 (over z, y, core).
Axes of the slice: x: 2, y: 2, z: 4, core: 2. Of those that a mesh axis runs over, the one named last changes fastest.
Arguments:
- hidden_in: bfloat16 [2, 1024, 2048], P(None, ('grp', 'ep')), parts along dimension 1, may hold values from -12 to 12
- expert_ids: int32 [2, 1024, 8], P(None, ('grp', 'ep')), parts along dimension 1, may hold values from 0 to 15, all different within a row; in each aligned block of 32 rows (0 to 31, 32 to 63, ..., all dimensions but the last counted through in order) at most 32 rows name the same one
- route_share: int32 [2, 1024, 8], P(None, ('grp', 'ep')), parts along dimension 1, may hold values from 4 to 28
- norm_gain: float32 [2048], replicated, may hold values from 0.1 to 1.9
- gate_weight: bfloat16 [16, 2048, 768], P('ep'), may hold values from -0.125 to 0.125
- up_weight: bfloat16 [16, 2048, 768], P('ep'), may hold values from -0.125 to 0.125
- down_weight: bfloat16 [16, 768, 2048], P('ep'), may hold values from -0.21875 to 0.21875
- exponent_table: int32 [16, 3, 6], P('ep'), may hold values from -2 to 1
Outputs:
- mixed_out: bfloat16 [2, 1024, 2048], P(None, ('grp', 'ep')), parts along dimension 1
The draws below stay inside these ranges and needn't reach their ends.
There are 2 independent parts, one for each index of `grp`. The reference program is written for one: setup_inputs(seed, part) draws one part's arguments, and reference() takes and returns one part's arrays. A program takes and returns all parts, laid end to end along the dimension named above; an argument that names none is the same for every part. Nothing has to cross between parts.
Inputs may be any that keep to these rules, and one draw needn't show every extreme that they name: `expert_ids`: each row names 8 different experts. Within each micro-batch, in each aligned block of 32 rows, no expert is named by more than 32 rows, and in some blocks one expert is named by exactly 32 rows.
All inputs are finite; a program needn't handle non-finite values.
Results may differ from the reference program's by a relative error of at most 0.0044.
Values may be sent and summed in bfloat16 or wider, within the bound.
No kernel may reach another device: no remote copies, remote signals or barrier semaphores. Data moves between devices by JAX's collectives and lax.ppermute only.
A program may use at most 64 MiB of HBM per device.

```python
import math
import jax
import jax.numpy as jnp
import numpy as np
from jax import lax

D = 2048
FF = 768
TOP = 8
SCALE_GROUP = 128
MICRO = 2
ROWS_DEV = 32
EXPERTS = 16
ROWS = 512
CAP = 32
N_EP = 16


def draw_hidden_in(key, part):
    key_base, key_rows, key_cols = jax.random.split(jax.random.fold_in(key, 17), 3)
    row_scale = jnp.exp(jax.random.uniform(key_rows, (MICRO, ROWS, 1), jnp.float32, math.log(0.3), math.log(3.0)))
    col_scale = jnp.exp(jax.random.uniform(key_cols, (1, 1, D), jnp.float32, math.log(0.5), math.log(2.0)))
    base = jax.random.normal(key_base, (MICRO, ROWS, D), jnp.float32)
    values = jnp.clip(base * row_scale * col_scale, -12.0, 12.0)
    return values.astype(jnp.bfloat16)


def touch_ends(result, own_key, low, largest):
    place = [jax.random.randint(jax.random.fold_in(own_key, axis), (), 0, length) for axis, length in enumerate(result.shape)]
    main_axis = result.shape.index(max(result.shape))
    beside = place[:main_axis] + [(place[main_axis] + 1) % result.shape[main_axis]] + place[main_axis + 1:]
    return result.at[tuple(place)].set(low).at[tuple(beside)].set(largest)


def steps_of(stream_key, dims, cuts, low, largest):
    def one(axis_at, parts):
        draws = jax.random.uniform(jax.random.fold_in(jax.random.fold_in(stream_key, 6), axis_at), (parts,), jnp.float32, low / len(cuts), largest / len(cuts))
        return jnp.repeat(jnp.exp(draws), dims[axis_at] // parts).reshape((-1,) + (1,) * (len(dims) - axis_at - 1))

    loudness = one(*cuts[0])
    for cut in cuts[1:]:
        loudness = loudness * one(*cut)
    return loudness


def assign_block(key, own, number, rows, count, top, most, lean):
    order = jax.random.permutation(key, count)
    crowded, common = load_shares(count, rows * top, most, lean, True), load_shares(count, rows * top, most, lean, False)
    places = jnp.arange(count)

    def named(tallies, offset_by):
        used = int((tallies > 0).sum())
        fixed = max(1, used // 4)
        passed = fixed + (places - fixed + offset_by * (used - fixed)) % max(1, count - fixed)
        return jnp.zeros((count,), jnp.int32).at[order[jnp.where(places < fixed, places, passed)]].set(jnp.asarray(tallies, jnp.int32))

    tallies = jnp.where(number % 4 == 0, named(crowded, number // 4), named(common, number - number // 4 - 1))
    mixed = jax.random.permutation(jax.random.fold_in(own, 3), count)
    source_of, sink = mixed[0:count // 2 * 2:2], mixed[1:count // 2 * 2:2]
    room = jnp.minimum(tallies[source_of] - 1, most - tallies[sink]) // 2
    room = jnp.where((source_of == order[0]) | (sink == order[0]) | (tallies[sink] == 0), 0, jnp.maximum(room, 0))
    passed = jax.random.randint(jax.random.fold_in(own, 4), (count // 2,), 0, 1 << 20) % (room + 1)
    tallies = tallies.at[source_of].add(-passed).at[sink].add(passed)
    members = jnp.searchsorted(jnp.cumsum(tallies), jnp.arange(rows * top), side="right").astype(jnp.int32)
    table = members.reshape(top, rows).T
    table = table[jax.random.permutation(jax.random.fold_in(own, 1), rows)]
    offset_by = jax.random.randint(jax.random.fold_in(own, 2), (rows, 1), 0, top)
    return jnp.take_along_axis(table, (jnp.arange(top)[None, :] + offset_by) % top, axis=1)


def load_shares(count, total, reach, lean, full):
    weights = [(1 << 20) // math.isqrt(rank ** lean) + 1 for rank in range(1, count + 1)]
    largest = reach if full else min(reach, max(-(-total // count), total * weights[0] // sum(weights)))
    least = 1 if total - largest >= count - 1 else 0
    given, surplus = [largest] + [least] * (count - 1), total - largest - least * (count - 1)
    while surplus > 0:
        free = [i for i in range(1, count) if given[i] < largest] or [i for i in range(1, count) if given[i] < reach]
        pool, remaining = sum([weights[i] for i in free]), surplus
        for i in free:
            extra = min(reach - given[i], max(1, remaining * weights[i] // pool), surplus)
            given[i] = given[i] + extra
            surplus = surplus - extra
    return np.array(given)


def gaussian(stream_key, extent, scale, most, shards=(), kind=jnp.bfloat16):
    values = jax.random.normal(stream_key, extent, jnp.float32) * scale
    if len(shards) > 0:
        values = steps_of(stream_key, extent, shards, -0.22, 0.18) * values
    return jnp.clip(values, min=-most, max=most).astype(kind)


def setup_inputs(seed: int = 0, part: int = 0) -> dict:
    splits = jax.random.split(jax.random.key(seed), 9)
    part_keys = jax.random.split(jax.random.fold_in(splits[8], part), 9)
    hidden_in = draw_hidden_in(jax.random.fold_in(jax.random.fold_in(splits[8], part), 71), part)
    expert_ids_keys = jax.random.split(jax.random.fold_in(part_keys[1], 1), MICRO * ROWS // ROWS_DEV)
    expert_ids_turns = jax.random.permutation(jax.random.fold_in(part_keys[1], 3), MICRO * ROWS // ROWS_DEV)
    expert_ids = jax.vmap(lambda own, number: assign_block(jax.random.fold_in(part_keys[1], 2), own, number, ROWS_DEV, EXPERTS, TOP, CAP, 2))(expert_ids_keys, expert_ids_turns).reshape((MICRO, ROWS, TOP))
    route_share = touch_ends(jax.random.randint(part_keys[2], (MICRO, ROWS, TOP), 4, 29), jax.random.fold_in(part_keys[2], 1), 4, 28).astype(jnp.int32)
    norm_gain = jnp.clip(1.0 + 0.18 * jax.random.normal(splits[3], (D,), jnp.float32), 0.1, 1.9)
    gate_weight = gaussian(splits[4], (EXPERTS, D, FF), D ** -0.5, 0.125, ((0, 16),))
    up_weight = gaussian(splits[5], (EXPERTS, D, FF), D ** -0.5, 0.125, ((0, 16),))
    down_weight = gaussian(splits[6], (EXPERTS, FF, D), FF ** -0.5, 0.21875, ((0, 16),))
    exponent_table = touch_ends(jax.random.randint(splits[7], (EXPERTS, 3, FF // SCALE_GROUP), -2, 2), jax.random.fold_in(splits[7], 1), -2, 1).astype(jnp.int32)
    return {"hidden_in": hidden_in, "expert_ids": expert_ids, "route_share": route_share, "norm_gain": norm_gain, "gate_weight": gate_weight, "up_weight": up_weight, "down_weight": down_weight, "exponent_table": exponent_table}


def normalize(hidden_in, norm_gain):
    values = hidden_in.astype(jnp.float32)
    power = lax.optimization_barrier(jnp.mean(values * values, axis=-1, keepdims=True))
    return (values * lax.rsqrt(power + 1e-06) * norm_gain.astype(jnp.float32)).astype(jnp.bfloat16)

def expert_ffn(operands):
    block_of_rows, gate_matrix, up_matrix, down_mat, scale_exponents = operands
    scale_factors = jnp.repeat(jnp.exp2(scale_exponents.astype(jnp.float32)), SCALE_GROUP, axis=1)
    gate_output = jnp.dot(block_of_rows, gate_matrix, preferred_element_type=jnp.float32) * scale_factors[0]
    up_output = jnp.dot(block_of_rows, up_matrix, preferred_element_type=jnp.float32) * scale_factors[1]
    hidden_state = (jax.nn.silu(gate_output) * up_output * scale_factors[2]).astype(jnp.bfloat16)
    return jnp.dot(hidden_state, down_mat, preferred_element_type=jnp.float32).astype(jnp.bfloat16)

def slot_places(chosen):
    grouped = chosen.reshape(N_EP, ROWS_DEV * TOP)
    onehot = (grouped[:, :, None] == jnp.arange(EXPERTS, dtype=jnp.int32)[None, None, :]).astype(jnp.int32)
    running = jnp.cumsum(onehot, axis=1) - 1
    position = lax.optimization_barrier(jnp.sum(running * onehot, axis=2)).astype(jnp.int32)
    return position.reshape(ROWS, TOP)

def reference(hidden_in, expert_ids, route_share, norm_gain, gate_weight, up_weight, down_weight, exponent_table):
    outputs = []
    for batch in range(MICRO):
        rows_in = hidden_in[batch]
        chosen = expert_ids[batch].astype(jnp.int32)
        normed = normalize(rows_in, norm_gain)
        position = slot_places(chosen)
        source = (jnp.arange(ROWS, dtype=jnp.int32) // ROWS_DEV)[:, None]
        column = (source * CAP + position).astype(jnp.int32)
        spread_rows = jnp.broadcast_to(normed[:, None, :], (ROWS, TOP, D))
        buffer = jnp.zeros((EXPERTS, N_EP * CAP, D), jnp.bfloat16).at[chosen, column].set(spread_rows)
        results = lax.map(expert_ffn, (buffer, gate_weight, up_weight, down_weight, exponent_table))
        picked = results[chosen, column]
        shares = route_share[batch].astype(jnp.float32) / 64.0
        mixed = jnp.einsum('rk,rkd->rd', shares, picked.astype(jnp.float32))
        outputs.append((rows_in.astype(jnp.float32) + mixed).astype(jnp.bfloat16))
    return jnp.stack(outputs)
```

```python
import jax
import jax.numpy as jnp
from jax import lax
from jax.sharding import PartitionSpec as P


def normalize(rows_in, norm_gain):
    values = rows_in.astype(jnp.float32)
    power = jnp.mean(values * values, axis=-1, keepdims=True)
    return (values * lax.rsqrt(power + 1e-06) * norm_gain).astype(jnp.bfloat16)


def local(
    hidden_in,
    expert_ids,
    route_share,
    norm_gain,
    gate_weight,
    up_weight,
    down_weight,
    exponent_table,
):
    owners = lax.axis_size("ep")
    batches, dev_rows, fanout = expert_ids.shape
    model_width = hidden_in.shape[2]
    groups = exponent_table.shape[2]
    scale_group = gate_weight.shape[2] // groups
    scale_factors = jnp.repeat(jnp.exp2(exponent_table[0].astype(jnp.float32)), scale_group, axis=1)
    gate_matrix = gate_weight[0]
    up_matrix = up_weight[0]
    down_mat = down_weight[0]

    extra = -(-owners // 128) * 128
    columns = jnp.arange(extra, dtype=jnp.int32)
    shares = route_share.astype(jnp.float32) / 64.0
    dense = jnp.sum(
        jnp.where(expert_ids[..., None] == columns, shares[..., None], 0.0), axis=2
    ).astype(jnp.bfloat16)
    payload = jnp.concatenate([normalize(hidden_in, norm_gain), dense], axis=2)
    mine = (columns == lax.axis_index("ep")).astype(jnp.float32)

    gathered = [lax.all_gather(payload[batch], "ep", axis=0, tiled=True) for batch in range(batches)]
    outputs = []
    for batch in range(batches):
        rows = gathered[batch][:, :model_width]
        weight = jnp.sum(gathered[batch][:, model_width:].astype(jnp.float32) * mine, axis=1)
        gate = jnp.dot(rows, gate_matrix, preferred_element_type=jnp.float32) * scale_factors[0]
        up = jnp.dot(rows, up_matrix, preferred_element_type=jnp.float32) * scale_factors[1]
        hidden = (jax.nn.silu(gate) * up * scale_factors[2]).astype(jnp.bfloat16)
        partial = jnp.dot(hidden, down_mat, preferred_element_type=jnp.float32)
        partial = (partial * weight[:, None]).astype(jnp.bfloat16)
        mixed = lax.psum_scatter(partial, "ep", scatter_dimension=0, tiled=True)
        outputs.append(hidden_in[batch].astype(jnp.float32) + mixed.astype(jnp.float32))
    return jnp.stack(outputs).astype(jnp.bfloat16)


def solution(mesh):
    return jax.shard_map(
        local,
        mesh=mesh,
        in_specs=(
            P(None, ("grp", "ep"), None),
            P(None, ("grp", "ep"), None),
            P(None, ("grp", "ep"), None),
            P(),
            P("ep", None, None),
            P("ep", None, None),
            P("ep", None, None),
            P("ep", None, None),
        ),
        out_specs=P(None, ("grp", "ep"), None),
        check_vma=False,
    )
```

```python
import jax
import jax.numpy as jnp
from jax import lax
from jax.sharding import PartitionSpec as P


def normalize(rows_in, norm_gain):
    values = rows_in.astype(jnp.float32)
    power = jnp.mean(values * values, axis=-1, keepdims=True)
    return (values * lax.rsqrt(power + 1e-06) * norm_gain).astype(jnp.bfloat16)


def local(
    hidden_in,
    expert_ids,
    route_share,
    norm_gain,
    gate_weight,
    up_weight,
    down_weight,
    exponent_table,
):
    owners = lax.axis_size("ep")
    batches, dev_rows, fanout = expert_ids.shape
    model_width = hidden_in.shape[2]
    groups = exponent_table.shape[2]
    scale_group = gate_weight.shape[2] // groups
    scale_factors = jnp.repeat(jnp.exp2(exponent_table[0].astype(jnp.float32)), scale_group, axis=1)
    gate_matrix = gate_weight[0]
    up_matrix = up_weight[0]
    down_mat = down_weight[0]

    extra = -(-owners // 128) * 128
    columns = jnp.arange(extra, dtype=jnp.int32)
    shares = route_share.astype(jnp.float32) / 64.0
    dense = jnp.sum(
        jnp.where(expert_ids[..., None] == columns, shares[..., None], 0.0), axis=2
    ).astype(jnp.bfloat16)
    payload = jnp.concatenate([normalize(hidden_in, norm_gain), dense], axis=2)
    mine = (columns == lax.axis_index("ep")).astype(jnp.float32)

    line = owners // 4

    def along_line(k):
        return [(i, (i + 4 * k) % owners) for i in range(owners)]

    across_mid = [(i, i ^ 2) for i in range(owners)]
    across_core = [(i, i ^ 1) for i in range(owners)]

    def gather(rows):
        pieces = [rows] + [lax.ppermute(rows, "ep", along_line(k)) for k in range(1, line)]
        here = jnp.concatenate(pieces, axis=0)
        there = lax.ppermute(here, "ep", across_mid)
        return [
            here,
            there,
            lax.ppermute(here, "ep", across_core),
            lax.ppermute(there, "ep", across_core),
        ]

    def add(a, b):
        return (a.astype(jnp.float32) + b.astype(jnp.float32)).astype(jnp.bfloat16)

    def scatter(parts):
        mid_sum = add(parts[1], lax.ppermute(parts[3], "ep", across_core))
        back = lax.ppermute(mid_sum, "ep", across_mid)
        total = add(add(parts[0], lax.ppermute(parts[2], "ep", across_core)), back)
        result = total[:dev_rows].astype(jnp.float32)
        for k in range(1, line):
            piece = total[k * dev_rows : (k + 1) * dev_rows]
            result = result + lax.ppermute(piece, "ep", along_line(line - k)).astype(jnp.float32)
        return result

    gathered = [gather(payload[batch]) for batch in range(batches)]
    outputs = []
    for batch in range(batches):
        both = jnp.concatenate(gathered[batch], axis=0)
        rows = both[:, :model_width]
        weight = jnp.sum(both[:, model_width:].astype(jnp.float32) * mine, axis=1)
        gate = jnp.dot(rows, gate_matrix, preferred_element_type=jnp.float32) * scale_factors[0]
        up = jnp.dot(rows, up_matrix, preferred_element_type=jnp.float32) * scale_factors[1]
        hidden = (jax.nn.silu(gate) * up * scale_factors[2]).astype(jnp.bfloat16)
        partial = jnp.dot(hidden, down_mat, preferred_element_type=jnp.float32)
        partial = (partial * weight[:, None]).astype(jnp.bfloat16)
        quarter = line * dev_rows
        mixed = scatter([partial[q * quarter : (q + 1) * quarter] for q in range(4)])
        outputs.append(hidden_in[batch].astype(jnp.float32) + mixed)
    return jnp.stack(outputs).astype(jnp.bfloat16)


def solution(mesh):
    return jax.shard_map(
        local,
        mesh=mesh,
        in_specs=(
            P(None, ("grp", "ep"), None),
            P(None, ("grp", "ep"), None),
            P(None, ("grp", "ep"), None),
            P(),
            P("ep", None, None),
            P("ep", None, None),
            P("ep", None, None),
            P("ep", None, None),
        ),
        out_specs=P(None, ("grp", "ep"), None),
        check_vma=False,
    )
```

```python
import functools

import jax
import jax.numpy as jnp
from jax import lax
from jax.experimental import pallas as pl
from jax.experimental.pallas import tpu as pltpu
from jax.sharding import PartitionSpec as P

LANES = 128
VMEM = pl.BlockSpec(memory_space=pltpu.VMEM)
SMEM = pl.BlockSpec(memory_space=pltpu.SMEM)


def call(kernel, operands, specs, shapes, scratch=(), flops=0, name=None, vmem=8):
    moved = sum(a.size * a.dtype.itemsize for a in operands)
    moved += sum(s.size * s.dtype.itemsize for s in shapes)
    return pl.pallas_call(
        kernel,
        out_shape=shapes,
        in_specs=specs,
        out_specs=[VMEM] * len(shapes),
        scratch_shapes=list(scratch),
        cost_estimate=pl.CostEstimate(flops=flops, bytes_accessed=moved, transcendentals=0),
        compiler_params=pltpu.CompilerParams(vmem_limit_bytes=vmem << 20),
        name=name,
    )(*operands)


def prepare_kernel(hidden_ref, ids_ref, share_ref, gain_ref, *out_refs):
    batches, rows, width = hidden_ref.shape
    fanout = ids_ref.shape[1]
    extra = out_refs[0].shape[1] - width
    for batch in range(batches):
        values = hidden_ref[batch].astype(jnp.float32)
        power = jnp.mean(values * values, axis=-1, keepdims=True)
        normed = values * lax.rsqrt(power + 1e-06) * gain_ref[...]
        out_refs[batch][:, :width] = normed.astype(jnp.bfloat16)
        expert = lax.broadcasted_iota(jnp.int32, (extra, rows), 0)
        dense = jnp.zeros((extra, rows), jnp.float32)
        for k in range(fanout):
            share = share_ref[batch, k : k + 1, :].astype(jnp.float32) * (1.0 / 64.0)
            dense = dense + jnp.where(expert == ids_ref[batch, k : k + 1, :], share, 0.0)
        out_refs[batch][:, width:] = dense.T.astype(jnp.bfloat16)


def ffn_kernel(pieces, owner_ref, scale_ref, gate_ref, up_ref, down_ref, *refs):
    x_refs, out_refs, (x_all, hidden) = refs[:pieces], refs[pieces : 2 * pieces], refs[2 * pieces :]
    width, ff = gate_ref.shape[1:]
    group = ff // scale_ref.shape[1]
    starts = []
    at = 0
    for x_ref in x_refs:
        x_all[at : at + x_ref.shape[0], :] = x_ref[...]
        starts.append(at)
        at += x_ref.shape[0]
    step = 2 * group if ff % (2 * group) == 0 else group
    for f in range(0, ff, step):
        x = x_all[:, :width]
        gate = jnp.dot(x, gate_ref[0, :, f : f + step], preferred_element_type=jnp.float32)
        up = jnp.dot(x, up_ref[0, :, f : f + step], preferred_element_type=jnp.float32)
        for part in range(0, step, group):
            b = (f + part) // group
            g = gate[:, part : part + group] * scale_ref[0, b]
            u = up[:, part : part + group] * scale_ref[1, b]
            h = g / (1.0 + jnp.exp(-g)) * u * scale_ref[2, b]
            hidden[:, f + part : f + part + group] = h.astype(jnp.bfloat16)
    shares = x_all[:, width:].astype(jnp.float32)
    here = lax.broadcasted_iota(jnp.int32, shares.shape, 1) == owner_ref[0]
    weight = jnp.sum(jnp.where(here, shares, 0.0), axis=1, keepdims=True)
    cols = 512 if width % 512 == 0 else LANES
    for n in range(0, width, cols):
        out = jnp.dot(hidden[...], down_ref[0, :, n : n + cols], preferred_element_type=jnp.float32)
        out = (out * weight).astype(jnp.bfloat16)
        for start, out_ref in zip(starts, out_refs):
            out_ref[:, n : n + cols] = out[start : start + out_ref.shape[0], :]


def ffn(xs, owner, scales, weights):
    rows = sum(x.shape[0] for x in xs)
    width, ff = weights[0].shape[1:]
    return call(
        functools.partial(ffn_kernel, len(xs)),
        [owner, scales, *weights, *xs],
        [SMEM, SMEM] + [VMEM] * (3 + len(xs)),
        [jax.ShapeDtypeStruct((x.shape[0], width), jnp.bfloat16) for x in xs],
        [pltpu.VMEM((rows, xs[0].shape[1]), jnp.bfloat16), pltpu.VMEM((rows, ff), jnp.bfloat16)],
        flops=6 * rows * width * ff,
        name="ffn",
        vmem=16,
    )


def join_kernel(*refs):
    at = 0
    for ref in refs[:-1]:
        refs[-1][at : at + ref.shape[0], :] = ref[...]
        at += ref.shape[0]


def join(pieces):
    rows = sum(p.shape[0] for p in pieces)
    shape = jax.ShapeDtypeStruct((rows, pieces[0].shape[1]), pieces[0].dtype)
    return call(join_kernel, pieces, [VMEM] * len(pieces), [shape], name="join")[0]


def add_kernel(terms, *refs):
    at = 0
    for out_ref in refs[terms:]:
        rows = slice(at, at + out_ref.shape[0])
        total = refs[0][rows, :].astype(jnp.float32)
        for ref in refs[1:terms]:
            total = total + ref[rows, :].astype(jnp.float32)
        out_ref[...] = total.astype(out_ref.dtype)
        at += out_ref.shape[0]


def add(terms, cuts=1):
    rows, width = terms[0].shape
    shape = jax.ShapeDtypeStruct((rows // cuts, width), terms[0].dtype)
    return call(
        functools.partial(add_kernel, len(terms)), terms, [VMEM] * len(terms), [shape] * cuts, name="add"
    )


def finish_kernel(terms, hidden_ref, *refs):
    out_ref = refs[-1]
    for batch in range(hidden_ref.shape[0]):
        total = hidden_ref[batch].astype(jnp.float32)
        mine = refs[batch * terms : (batch + 1) * terms]
        mixed = mine[0][...].astype(jnp.float32)
        for ref in mine[1:]:
            mixed = mixed + ref[...].astype(jnp.float32)
        out_ref[batch] = (total + mixed).astype(out_ref.dtype)


def finish(hidden_in, terms):
    flat = [t for batch in terms for t in batch]
    return call(
        functools.partial(finish_kernel, len(terms[0])),
        [hidden_in, *flat],
        [VMEM] * (1 + len(flat)),
        [jax.ShapeDtypeStruct(hidden_in.shape, hidden_in.dtype)],
        name="finish",
    )[0]


def local(
    hidden_in,
    expert_ids,
    route_share,
    norm_gain,
    gate_weight,
    up_weight,
    down_weight,
    exponent_table,
):
    owners = lax.axis_size("ep")
    batches, dev_rows, fanout = expert_ids.shape
    model_width = hidden_in.shape[2]
    extra = -(-owners // LANES) * LANES
    weights = (gate_weight, up_weight, down_weight)
    scales = jnp.exp2(exponent_table[0].astype(jnp.float32))
    owner = lax.axis_index("ep").astype(jnp.int32).reshape(1)

    line = owners // 4

    def along_line(rows, k):
        return lax.ppermute(rows, "ep", [(i, (i + 4 * k) % owners) for i in range(owners)])

    def to_mid(rows):
        return lax.ppermute(rows, "ep", [(i, i ^ 2) for i in range(owners)])

    def to_core(rows):
        return lax.ppermute(rows, "ep", [(i, i ^ 1) for i in range(owners)])

    payload = call(
        prepare_kernel,
        [
            hidden_in,
            expert_ids.transpose(0, 2, 1),
            route_share.transpose(0, 2, 1),
            norm_gain.reshape(1, model_width),
        ],
        [VMEM] * 4,
        [jax.ShapeDtypeStruct((dev_rows, model_width + extra), jnp.bfloat16)] * batches,
        name="prepare",
    )

    terms = []
    pieces = None
    for rows in payload:
        if pieces is not None:
            rows, *pieces = lax.optimization_barrier((rows, *pieces))
        pieces = [rows] + [along_line(rows, k) for k in range(1, line)]
        here = join(pieces)
        there = to_mid(here)
        out_here, out_here_core = ffn([here, to_core(here)], owner, scales, weights)
        out_there, out_there_core = ffn([there, to_core(there)], owner, scales, weights)
        back = to_mid(add([out_there, to_core(out_there_core)])[0])
        total = add([out_here, to_core(out_here_core), back], line)
        terms.append([total[0]] + [along_line(total[k], line - k) for k in range(1, line)])
    return finish(hidden_in, terms)


def solution(mesh):
    return jax.shard_map(
        local,
        mesh=mesh,
        in_specs=(
            P(None, ("grp", "ep"), None),
            P(None, ("grp", "ep"), None),
            P(None, ("grp", "ep"), None),
            P(),
            P("ep", None, None),
            P("ep", None, None),
            P("ep", None, None),
            P("ep", None, None),
        ),
        out_specs=P(None, ("grp", "ep"), None),
        check_vma=False,
    )
```

```python
import functools

import jax
import jax.numpy as jnp
from jax import lax
from jax.experimental import pallas as pl
from jax.experimental.pallas import tpu as pltpu
from jax.sharding import PartitionSpec as P

LANES = 128
VMEM = pl.BlockSpec(memory_space=pltpu.VMEM)
SMEM = pl.BlockSpec(memory_space=pltpu.SMEM)
HBM = pl.BlockSpec(memory_space=pltpu.HBM)
PARTS = 2


def call(kernel, operands, specs, shapes, scratch=(), flops=0, name=None, vmem=8):
    moved = sum(a.size * a.dtype.itemsize for a in operands)
    moved += sum(s.size * s.dtype.itemsize for s in shapes)
    return pl.pallas_call(
        kernel,
        out_shape=shapes,
        in_specs=specs,
        out_specs=[VMEM] * len(shapes),
        scratch_shapes=list(scratch),
        cost_estimate=pl.CostEstimate(flops=flops, bytes_accessed=moved, transcendentals=0),
        compiler_params=pltpu.CompilerParams(vmem_limit_bytes=vmem << 20),
        name=name,
    )(*operands)


def after(value, *others):
    return lax.optimization_barrier((value, *others))[0]


def prepare_kernel(hidden_hbm, ids_hbm, share_hbm, gain_hbm, *refs):
    out_refs, (hidden_ref, ids_ref, share_ref, gain_ref, sems) = refs[:-5], refs[-5:]
    sources = (hidden_hbm, ids_hbm, share_hbm, gain_hbm)
    targets = (hidden_ref, ids_ref, share_ref, gain_ref)
    copies = [pltpu.make_async_copy(s, t, sems.at[i]) for i, (s, t) in enumerate(zip(sources, targets))]
    for copy in copies:
        copy.start()
    for copy in copies:
        copy.wait()
    batches, rows, width = hidden_ref.shape
    fanout = ids_ref.shape[1]
    line, part, full = out_refs[0].shape
    extra = full - width
    parts = rows // part
    for batch in range(batches):
        values = hidden_ref[batch].astype(jnp.float32)
        power = jnp.mean(values * values, axis=-1, keepdims=True)
        normed = (values * lax.rsqrt(power + 1e-06) * gain_ref[...]).astype(jnp.bfloat16)
        expert = lax.broadcasted_iota(jnp.int32, (extra, rows), 0)
        dense = jnp.zeros((extra, rows), jnp.float32)
        for k in range(fanout):
            share = share_ref[batch, k : k + 1, :].astype(jnp.float32) * (1.0 / 64.0)
            dense = dense + jnp.where(expert == ids_ref[batch, k : k + 1, :], share, 0.0)
        dense = dense.T.astype(jnp.bfloat16)
        for p in range(parts):
            out_ref = out_refs[batch * parts + p]
            for place in range(line):
                out_ref[place, :, :width] = normed[p * part : (p + 1) * part]
                out_ref[place, :, width:] = dense[p * part : (p + 1) * part]


def load_kernel(*refs):
    count = len(refs) // 2
    copies = [pltpu.make_async_copy(refs[i], refs[count + i], refs[-1].at[i]) for i in range(count)]
    for copy in copies:
        copy.start()
    for copy in copies:
        copy.wait()


def load(weights):
    return call(
        load_kernel,
        weights,
        [HBM] * len(weights),
        [jax.ShapeDtypeStruct(w.shape, w.dtype) for w in weights],
        [pltpu.SemaphoreType.DMA((len(weights),))],
        name="load",
    )


def ffn_kernel(owner_ref, scale_ref, gate_ref, up_ref, down_ref, *refs):
    x_refs, (mine_ref, other_ref, x_all, hidden) = refs[:4], refs[4:]
    width, ff = gate_ref.shape[1:]
    group = ff // scale_ref.shape[1]
    line, part, full = x_refs[0].shape
    rows = line * part
    for i, x_ref in enumerate(x_refs):
        x_all[i * rows : (i + 1) * rows, :] = x_ref[...].reshape(rows, full)
    step = 2 * group if ff % (2 * group) == 0 else group
    for f in range(0, ff, step):
        x = x_all[:, :width]
        gate = jnp.dot(x, gate_ref[0, :, f : f + step], preferred_element_type=jnp.float32)
        up = jnp.dot(x, up_ref[0, :, f : f + step], preferred_element_type=jnp.float32)
        for at in range(0, step, group):
            b = (f + at) // group
            g = gate[:, at : at + group] * scale_ref[0, b]
            u = up[:, at : at + group] * scale_ref[1, b]
            h = g / (1.0 + jnp.exp(-g)) * u * scale_ref[2, b]
            hidden[:, f + at : f + at + group] = h.astype(jnp.bfloat16)
    shares = x_all[:, width:].astype(jnp.float32)
    here = lax.broadcasted_iota(jnp.int32, shares.shape, 1) == owner_ref[0]
    weight = jnp.sum(jnp.where(here, shares, 0.0), axis=1, keepdims=True)
    cols = 512 if width % 512 == 0 else LANES
    for n in range(0, width, cols):
        out = jnp.dot(hidden[...], down_ref[0, :, n : n + cols], preferred_element_type=jnp.float32)
        out = (out * weight).astype(jnp.bfloat16).reshape(4, line, part, cols)
        mine_ref[:, :, :, n : n + cols] = out[:2]
        other_ref[:, :, :, n : n + cols] = out[2:]


def ffn(xs, owner, scales, weights):
    line, part, full = xs[0].shape
    width, ff = weights[0].shape[1:]
    rows = 4 * line * part
    return call(
        ffn_kernel,
        [owner, scales, *weights, *xs],
        [SMEM, SMEM] + [VMEM] * 7,
        [jax.ShapeDtypeStruct((2, line, part, width), jnp.bfloat16)] * 2,
        [pltpu.VMEM((rows, full), jnp.bfloat16), pltpu.VMEM((rows, ff), jnp.bfloat16)],
        flops=6 * rows * width * ff,
        name="ffn",
        vmem=16,
    )


def add_kernel(slot, mine_ref, other_ref, *refs):
    out_ref = refs[-1]
    for place in range(out_ref.shape[0]):
        total = mine_ref[slot, place].astype(jnp.float32) + other_ref[slot, place].astype(jnp.float32)
        for ref in refs[:-1]:
            total = total + ref[place].astype(jnp.float32)
        out_ref[place] = total.astype(out_ref.dtype)


def add(slot, mine, other, *more):
    shape = jax.ShapeDtypeStruct(mine.shape[1:], mine.dtype)
    return call(
        functools.partial(add_kernel, slot),
        [mine, other, *more],
        [VMEM] * (2 + len(more)),
        [shape],
        name="add",
    )[0]


def finish_kernel(hidden_ref, *refs):
    term_refs, out_ref = refs[:-1], refs[-1]
    batches, rows, _ = hidden_ref.shape
    part = term_refs[0].shape[1]
    parts = rows // part
    for batch in range(batches):
        for p in range(parts):
            at = slice(p * part, (p + 1) * part)
            term_ref = term_refs[batch * parts + p]
            mixed = term_ref[0].astype(jnp.float32)
            for place in range(1, term_ref.shape[0]):
                mixed = mixed + term_ref[place].astype(jnp.float32)
            total = hidden_ref[batch, at].astype(jnp.float32) + mixed
            out_ref[batch, at] = total.astype(out_ref.dtype)


def finish(hidden_in, terms):
    return call(
        finish_kernel,
        [hidden_in, *terms],
        [VMEM] * (1 + len(terms)),
        [jax.ShapeDtypeStruct(hidden_in.shape, hidden_in.dtype)],
        name="finish",
    )[0]


def local(
    hidden_in,
    expert_ids,
    route_share,
    norm_gain,
    gate_weight,
    up_weight,
    down_weight,
    exponent_table,
):
    owners = lax.axis_size("ep")
    batches, dev_rows, fanout = expert_ids.shape
    model_width = hidden_in.shape[2]
    extra = -(-owners // LANES) * LANES
    parts = PARTS if dev_rows % (16 * PARTS) == 0 else 1
    part = dev_rows // parts
    scales = jnp.exp2(exponent_table[0].astype(jnp.float32))
    owner = lax.axis_index("ep").astype(jnp.int32).reshape(1)

    line = owners // 4
    lines = [[4 * place + at for place in range(line)] for at in range(4)]

    def over_line(rows):
        return lax.all_to_all(rows, "ep", 0, 0, axis_index_groups=lines, tiled=True)

    def to_mid(rows):
        return lax.ppermute(rows, "ep", [(i, i ^ 2) for i in range(owners)])

    def to_core(rows):
        return lax.ppermute(rows, "ep", [(i, i ^ 1) for i in range(owners)])

    operands = [
        hidden_in,
        expert_ids.transpose(0, 2, 1),
        route_share.transpose(0, 2, 1),
        norm_gain.reshape(1, model_width),
    ]
    payload = call(
        prepare_kernel,
        operands,
        [HBM] * 4,
        [jax.ShapeDtypeStruct((line, part, model_width + extra), jnp.bfloat16)] * (batches * parts),
        [pltpu.VMEM(a.shape, a.dtype) for a in operands] + [pltpu.SemaphoreType.DMA((4,))],
        name="prepare",
    )
    weights = load([gate_weight, up_weight, down_weight])

    count = len(payload)
    here, there, here_core = {}, {}, {}
    mine, other, back = {}, {}, {}
    sent = {}
    terms = {}

    def expert(s):
        order = (sent[s - 1],) if s > 0 else ()
        rows = after(there[s], *order)
        mine[s], out_other = ffn([here[s], rows, here_core[s], to_core(rows)], owner, scales, weights)
        other[s] = to_core(out_other)
        sent[s] = add(1, mine[s], other[s])
        back[s] = to_mid(sent[s])

    def give_back(s):
        last = min(s + 1, count - 1)
        total = add(0, mine[s], other[s], after(back[s], sent[last]))
        terms[s] = over_line(total)

    for t in range(count + 4):
        if t < count:
            order = (here[t - 1],) if t > 0 else (payload[0],)
            here[t] = over_line(after(payload[t], *order))
            if t == 0:
                here[t] = after(here[t], *weights)
            elif t >= 3:
                here[t] = after(here[t], sent[t - 3])
            there[t] = to_mid(here[t])
            here_core[t] = to_core(here[t])
        if 0 <= t - 1 < count:
            expert(t - 1)
        if 0 <= t - 3 < count:
            give_back(t - 3)
    return finish(hidden_in, [terms[s] for s in range(count)])


def solution(mesh):
    return jax.shard_map(
        local,
        mesh=mesh,
        in_specs=(
            P(None, ("grp", "ep"), None),
            P(None, ("grp", "ep"), None),
            P(None, ("grp", "ep"), None),
            P(),
            P("ep", None, None),
            P("ep", None, None),
            P("ep", None, None),
            P("ep", None, None),
        ),
        out_specs=P(None, ("grp", "ep"), None),
        check_vma=False,
    )
```

```python
import functools

import jax
import jax.numpy as jnp
from jax import lax
from jax.experimental import pallas as pl
from jax.experimental.pallas import tpu as pltpu
from jax.sharding import PartitionSpec as P

LANES = 128
VMEM = pl.BlockSpec(memory_space=pltpu.VMEM)
SMEM = pl.BlockSpec(memory_space=pltpu.SMEM)
HBM = pl.BlockSpec(memory_space=pltpu.HBM)
ANY_VMEM = pl.BlockSpec(memory_space=pltpu.VMEM)
PARTS = 1


def call(kernel, operands, specs, shapes, scratch=(), flops=0, name=None, vmem=8, out_spec=VMEM):
    moved = sum(a.size * a.dtype.itemsize for a in operands)
    moved += sum(s.size * s.dtype.itemsize for s in shapes)
    if out_spec is VMEM:
        shapes = [pltpu.VMEM(s.shape, s.dtype) for s in shapes]
    pinned = {id(VMEM): pltpu.VMEM, id(HBM): pltpu.HBM}
    operands = [
        pltpu.with_memory_space_constraint(a, pinned[id(spec)]) if id(spec) in pinned else a
        for a, spec in zip(operands, specs)
    ]
    return pl.pallas_call(
        kernel,
        out_shape=shapes,
        in_specs=specs,
        out_specs=[out_spec] * len(shapes),
        scratch_shapes=list(scratch),
        cost_estimate=pl.CostEstimate(flops=flops, bytes_accessed=moved, transcendentals=0),
        compiler_params=pltpu.CompilerParams(vmem_limit_bytes=vmem << 20),
        name=name,
    )(*operands)


def after(value, *others):
    return lax.optimization_barrier((value, *others))[0]


def prepare_kernel(hidden_hbm, ids_hbm, share_hbm, gain_hbm, *refs):
    out_refs, (hidden_ref, ids_ref, share_ref, gain_ref, sems) = refs[:-5], refs[-5:]
    sources = (hidden_hbm, ids_hbm, share_hbm, gain_hbm)
    targets = (hidden_ref, ids_ref, share_ref, gain_ref)
    copies = [pltpu.make_async_copy(s, t, sems.at[i]) for i, (s, t) in enumerate(zip(sources, targets))]
    for copy in copies:
        copy.start()
    for copy in copies:
        copy.wait()
    batches, rows, width = hidden_ref.shape
    fanout = ids_ref.shape[1]
    part, full = out_refs[0].shape
    extra = full - width
    parts = rows // part
    for batch in range(batches):
        values = hidden_ref[batch].astype(jnp.float32)
        power = jnp.mean(values * values, axis=-1, keepdims=True)
        normed = (values * lax.rsqrt(power + 1e-06) * gain_ref[...]).astype(jnp.bfloat16)
        expert = lax.broadcasted_iota(jnp.int32, (extra, rows), 0)
        dense = jnp.zeros((extra, rows), jnp.float32)
        for k in range(fanout):
            share = share_ref[batch, k : k + 1, :].astype(jnp.float32) * (1.0 / 64.0)
            dense = dense + jnp.where(expert == ids_ref[batch, k : k + 1, :], share, 0.0)
        dense = dense.T.astype(jnp.bfloat16)
        for p in range(parts):
            out_ref = out_refs[batch * parts + p]
            out_ref[:, :width] = normed[p * part : (p + 1) * part]
            out_ref[:, width:] = dense[p * part : (p + 1) * part]


def load_kernel(*refs):
    count = len(refs) // 2
    copies = [pltpu.make_async_copy(refs[i], refs[count + i], refs[-1].at[i]) for i in range(count)]
    for copy in copies:
        copy.start()
    for copy in copies:
        copy.wait()


def load(weights):
    return call(
        load_kernel,
        weights,
        [HBM] * len(weights),
        [jax.ShapeDtypeStruct(w.shape, w.dtype) for w in weights],
        [pltpu.SemaphoreType.DMA((len(weights),))],
        name="load",
    )


def join_kernel(*refs):
    for place, ref in enumerate(refs[:-1]):
        refs[-1][place] = ref[...]


def join(pieces):
    shape = jax.ShapeDtypeStruct((len(pieces), *pieces[0].shape), pieces[0].dtype)
    return call(join_kernel, pieces, [VMEM] * len(pieces), [shape], name="join")[0]


def ffn_kernel(owner_ref, scale_ref, gate_ref, up_ref, down_ref, *refs):
    x_refs, (mine_ref, other_ref, x_all, hidden) = refs[:4], refs[4:]
    width, ff = gate_ref.shape[1:]
    group = ff // scale_ref.shape[1]
    line, part, full = x_refs[0].shape
    rows = line * part
    for i, x_ref in enumerate(x_refs):
        x_all[i * rows : (i + 1) * rows, :] = x_ref[...].reshape(rows, full)
    step = 2 * group if ff % (2 * group) == 0 else group
    for f in range(0, ff, step):
        x = x_all[:, :width]
        gate = jnp.dot(x, gate_ref[0, :, f : f + step], preferred_element_type=jnp.float32)
        up = jnp.dot(x, up_ref[0, :, f : f + step], preferred_element_type=jnp.float32)
        for at in range(0, step, group):
            b = (f + at) // group
            g = gate[:, at : at + group] * scale_ref[0, b]
            u = up[:, at : at + group] * scale_ref[1, b]
            h = g / (1.0 + jnp.exp(-g)) * u * scale_ref[2, b]
            hidden[:, f + at : f + at + group] = h.astype(jnp.bfloat16)
    shares = x_all[:, width:].astype(jnp.float32)
    here = lax.broadcasted_iota(jnp.int32, shares.shape, 1) == owner_ref[0]
    weight = jnp.sum(jnp.where(here, shares, 0.0), axis=1, keepdims=True)
    cols = 512 if width % 512 == 0 else LANES
    for n in range(0, width, cols):
        out = jnp.dot(hidden[...], down_ref[0, :, n : n + cols], preferred_element_type=jnp.float32)
        out = (out * weight).astype(jnp.bfloat16).reshape(4, line, part, cols)
        mine_ref[:, :, :, n : n + cols] = out[:2]
        other_ref[:, :, :, n : n + cols] = out[2:]


def ffn(xs, owner, scales, weights):
    line, part, full = xs[0].shape
    width, ff = weights[0].shape[1:]
    rows = 4 * line * part
    return call(
        ffn_kernel,
        [owner, scales, *weights, *xs],
        [SMEM, SMEM] + [VMEM] * 7,
        [jax.ShapeDtypeStruct((2, line, part, width), jnp.bfloat16)] * 2,
        [pltpu.VMEM((rows, full), jnp.bfloat16), pltpu.VMEM((rows, ff), jnp.bfloat16)],
        flops=6 * rows * width * ff,
        name="ffn",
        vmem=16,
    )


def add_kernel(slot, mine_ref, other_ref, *refs):
    line = mine_ref.shape[1]
    if slot:
        more, outs = (), [refs[0].at[place] for place in range(line)]
    else:
        more, outs = refs[:1], refs[1:]
    for place, out_ref in enumerate(outs):
        total = mine_ref[slot, place].astype(jnp.float32) + other_ref[slot, place].astype(jnp.float32)
        for ref in more:
            total = total + ref[place].astype(jnp.float32)
        out_ref[...] = total.astype(out_ref.dtype)


def add_there(mine, other):
    shape = jax.ShapeDtypeStruct(mine.shape[1:], mine.dtype)
    return call(functools.partial(add_kernel, 1), [mine, other], [VMEM] * 2, [shape], name="add_there")[0]


def add_here(mine, other, back):
    shape = jax.ShapeDtypeStruct(mine.shape[2:], mine.dtype)
    return call(
        functools.partial(add_kernel, 0),
        [mine, other, back],
        [VMEM] * 3,
        [shape] * mine.shape[1],
        name="add_here",
    )


def finish_kernel(terms, hidden_ref, *refs):
    term_refs, out_ref = refs[:-1], refs[-1]
    batches, rows, _ = hidden_ref.shape
    part = term_refs[0].shape[0]
    parts = rows // part
    for batch in range(batches):
        for p in range(parts):
            at = slice(p * part, (p + 1) * part)
            first = (batch * parts + p) * terms
            mixed = term_refs[first][...].astype(jnp.float32)
            for ref in term_refs[first + 1 : first + terms]:
                mixed = mixed + ref[...].astype(jnp.float32)
            total = hidden_ref[batch, at].astype(jnp.float32) + mixed
            out_ref[batch, at] = total.astype(out_ref.dtype)


def finish(hidden_in, terms):
    flat = [t for mine in terms for t in mine]
    return call(
        functools.partial(finish_kernel, len(terms[0])),
        [hidden_in, *flat],
        [ANY_VMEM] + [VMEM] * len(flat),
        [jax.ShapeDtypeStruct(hidden_in.shape, hidden_in.dtype)],
        name="finish",
        out_spec=ANY_VMEM,
    )[0]


def local(
    hidden_in,
    expert_ids,
    route_share,
    norm_gain,
    gate_weight,
    up_weight,
    down_weight,
    exponent_table,
):
    owners = lax.axis_size("ep")
    batches, dev_rows, fanout = expert_ids.shape
    model_width = hidden_in.shape[2]
    extra = -(-owners // LANES) * LANES
    parts = PARTS if dev_rows % (16 * PARTS) == 0 else 1
    part = dev_rows // parts
    scales = jnp.exp2(exponent_table[0].astype(jnp.float32))
    owner = lax.axis_index("ep").astype(jnp.int32).reshape(1)

    line = owners // 4

    def along_line(rows, k):
        return lax.ppermute(rows, "ep", [(i, (i + 4 * k) % owners) for i in range(owners)])

    def over_line(rows):
        return join([rows] + [along_line(rows, k) for k in range(1, line)])

    def to_mid(rows):
        return lax.ppermute(rows, "ep", [(i, i ^ 2) for i in range(owners)])

    def to_core(rows):
        return lax.ppermute(rows, "ep", [(i, i ^ 1) for i in range(owners)])

    operands = [
        hidden_in,
        expert_ids.transpose(0, 2, 1),
        route_share.transpose(0, 2, 1),
        norm_gain.reshape(1, model_width),
    ]
    payload = call(
        prepare_kernel,
        operands,
        [HBM] * 4,
        [jax.ShapeDtypeStruct((part, model_width + extra), jnp.bfloat16)] * (batches * parts),
        [pltpu.VMEM(a.shape, a.dtype) for a in operands] + [pltpu.SemaphoreType.DMA((4,))],
        name="prepare",
    )
    weights = load([gate_weight, up_weight, down_weight])

    count = len(payload)
    here, there, here_core = {}, {}, {}
    mine, other, back = {}, {}, {}
    sent = {}
    terms = {}

    def expert(s):
        order = (sent[s - 1],) if s > 0 else ()
        rows = after(there[s], *order)
        mine[s], out_other = ffn([here[s], rows, here_core[s], to_core(rows)], owner, scales, weights)
        other[s] = to_core(out_other)
        sent[s] = add_there(mine[s], other[s])
        back[s] = to_mid(sent[s])

    def give_back(s):
        last = min(s + 1, count - 1)
        total = add_here(mine[s], other[s], after(back[s], sent[last]))
        terms[s] = [total[0]] + [along_line(total[k], line - k) for k in range(1, line)]

    for t in range(count + 4):
        if t < count:
            order = (here[t - 1],) if t > 0 else (payload[0],)
            here[t] = over_line(after(payload[t], *order))
            if t == 0:
                here[t] = after(here[t], *weights)
            elif t >= 3:
                here[t] = after(here[t], sent[t - 3])
            there[t] = to_mid(here[t])
            here_core[t] = to_core(here[t])
        if 0 <= t - 1 < count:
            expert(t - 1)
        if 0 <= t - 3 < count:
            give_back(t - 3)
    return finish(hidden_in, [terms[s] for s in range(count)])


def solution(mesh):
    return jax.shard_map(
        local,
        mesh=mesh,
        in_specs=(
            P(None, ("grp", "ep"), None),
            P(None, ("grp", "ep"), None),
            P(None, ("grp", "ep"), None),
            P(),
            P("ep", None, None),
            P("ep", None, None),
            P("ep", None, None),
            P("ep", None, None),
        ),
        out_specs=P(None, ("grp", "ep"), None),
        check_vma=False,
    )
```

```python
import functools

import jax
import jax.numpy as jnp
from jax import lax
from jax.experimental import pallas as pl
from jax.experimental.pallas import tpu as pltpu
from jax.sharding import PartitionSpec as P

LANES = 128
VMEM = pl.BlockSpec(memory_space=pltpu.VMEM)
HBM = pl.BlockSpec(memory_space=pltpu.HBM)
SMEM = pl.BlockSpec(memory_space=pltpu.SMEM)
PINNED = {pltpu.VMEM, pltpu.HBM}


def call(kernel, operands, specs, shapes, scratch=(), name=None, vmem=8, pin=True):
    if pin:
        shapes = [pltpu.VMEM(s.shape, s.dtype) for s in shapes]
        operands = [
            pltpu.with_memory_space_constraint(a, spec.memory_space)
            if spec.memory_space in PINNED
            else a
            for a, spec in zip(operands, specs)
        ]
    return pl.pallas_call(
        kernel,
        out_shape=shapes,
        in_specs=specs,
        out_specs=[VMEM] * len(shapes),
        scratch_shapes=list(scratch),
        cost_estimate=pl.CostEstimate(flops=0, bytes_accessed=0, transcendentals=0),
        compiler_params=pltpu.CompilerParams(vmem_limit_bytes=vmem << 20),
        name=name,
    )(*operands)


def after(value, *others):
    return lax.optimization_barrier((value, *others))[0]


def prepare_kernel(hidden_hbm, ids_hbm, share_hbm, gain_hbm, *refs):
    out_refs, (hidden_ref, ids_ref, share_ref, gain_ref, sems) = refs[:-5], refs[-5:]
    sources = (hidden_hbm, ids_hbm, share_hbm, gain_hbm)
    targets = (hidden_ref, ids_ref, share_ref, gain_ref)
    copies = [pltpu.make_async_copy(s, t, sems.at[i]) for i, (s, t) in enumerate(zip(sources, targets))]
    for copy in copies:
        copy.start()
    for copy in copies:
        copy.wait()
    rows, width = hidden_ref.shape[1:]
    fanout = ids_ref.shape[1]
    extra = out_refs[0].shape[2] - width
    for batch, out_ref in enumerate(out_refs):
        values = hidden_ref[batch].astype(jnp.float32)
        power = jnp.mean(values * values, axis=-1, keepdims=True)
        normed = values * lax.rsqrt(power + 1e-06) * gain_ref[...]
        out_ref[0, :, :width] = normed.astype(jnp.bfloat16)
        expert = lax.broadcasted_iota(jnp.int32, (extra, rows), 0)
        dense = jnp.zeros((extra, rows), jnp.float32)
        for k in range(fanout):
            share = share_ref[batch, k : k + 1, :].astype(jnp.float32) * (1.0 / 64.0)
            dense = dense + jnp.where(expert == ids_ref[batch, k : k + 1, :], share, 0.0)
        out_ref[0, :, width:] = dense.T.astype(jnp.bfloat16)


def prepare(hidden_in, expert_ids, route_share, norm_gain, extra):
    batches, rows, width = hidden_in.shape
    operands = [
        hidden_in,
        expert_ids.transpose(0, 2, 1),
        route_share.transpose(0, 2, 1),
        norm_gain.reshape(1, width),
    ]
    return call(
        prepare_kernel,
        operands,
        [HBM] * 4,
        [jax.ShapeDtypeStruct((1, rows, width + extra), jnp.bfloat16)] * batches,
        [pltpu.VMEM(a.shape, a.dtype) for a in operands] + [pltpu.SemaphoreType.DMA((4,))],
        name="prepare",
    )


def join_kernel(*refs):
    at = 0
    for ref in refs[:-1]:
        refs[-1][at : at + ref.shape[0]] = ref[...]
        at += ref.shape[0]


def join(a, b):
    shape = jax.ShapeDtypeStruct((a.shape[0] + b.shape[0], *a.shape[1:]), a.dtype)
    return call(join_kernel, [a, b], [VMEM] * 2, [shape], name="join")[0]


def ffn_kernel(owner_ref, scale_ref, gate_hbm, up_hbm, down_hbm, *refs):
    x_refs, (mine_ref, other_ref, gate_ref, up_ref, down_ref, x_all, hidden, sems) = refs[:4], refs[4:]
    width, ff = gate_ref.shape
    group = ff // scale_ref.shape[1]
    step = 2 * group if ff % (2 * group) == 0 else group
    steps = ff // step
    copies = []
    for i in range(steps):
        cut = slice(i * step, (i + 1) * step)
        copies.append(pltpu.make_async_copy(gate_hbm.at[0, :, cut], gate_ref.at[:, cut], sems.at[2 * i]))
        copies.append(pltpu.make_async_copy(up_hbm.at[0, :, cut], up_ref.at[:, cut], sems.at[2 * i + 1]))
    copies.append(pltpu.make_async_copy(down_hbm.at[0], down_ref, sems.at[2 * steps]))
    for copy in copies:
        copy.start()
    pieces, part, full = x_refs[0].shape
    rows = pieces * part
    for i, x_ref in enumerate(x_refs):
        x_all[i * rows : (i + 1) * rows, :] = x_ref[...].reshape(rows, full)
    for i in range(steps):
        cut = slice(i * step, (i + 1) * step)
        x = x_all[:, :width]
        copies[2 * i].wait()
        gate = jnp.dot(x, gate_ref[:, cut], preferred_element_type=jnp.float32)
        copies[2 * i + 1].wait()
        up = jnp.dot(x, up_ref[:, cut], preferred_element_type=jnp.float32)
        for at in range(0, step, group):
            b = (i * step + at) // group
            g = gate[:, at : at + group] * scale_ref[0, b]
            u = up[:, at : at + group] * scale_ref[1, b]
            h = g / (1.0 + jnp.exp(-g)) * u * scale_ref[2, b]
            hidden[:, i * step + at : i * step + at + group] = h.astype(jnp.bfloat16)
    shares = x_all[:, width:].astype(jnp.float32)
    here = lax.broadcasted_iota(jnp.int32, shares.shape, 1) == owner_ref[0]
    weight = jnp.sum(jnp.where(here, shares, 0.0), axis=1, keepdims=True)
    copies[2 * steps].wait()
    cols = 512 if width % 512 == 0 else LANES
    for n in range(0, width, cols):
        out = jnp.dot(hidden[...], down_ref[:, n : n + cols], preferred_element_type=jnp.float32)
        out = (out * weight).astype(jnp.bfloat16).reshape(4, pieces, part, cols)
        mine_ref[:, :, :, n : n + cols] = out[:2]
        other_ref[:, :, :, n : n + cols] = out[2:]


def ffn(xs, owner, scales, weights):
    pieces, part, full = xs[0].shape
    width, ff = weights[0].shape[1:]
    rows = 4 * pieces * part
    return call(
        ffn_kernel,
        [owner, scales, *weights, *xs],
        [SMEM, SMEM] + [HBM] * 3 + [VMEM] * 4,
        [jax.ShapeDtypeStruct((2, pieces, part, width), jnp.bfloat16)] * 2,
        [
            pltpu.VMEM((width, ff), jnp.bfloat16),
            pltpu.VMEM((width, ff), jnp.bfloat16),
            pltpu.VMEM((ff, width), jnp.bfloat16),
            pltpu.VMEM((rows, full), jnp.bfloat16),
            pltpu.VMEM((rows, ff), jnp.bfloat16),
            pltpu.SemaphoreType.DMA((2 * (ff // LANES) + 1,)),
        ],
        name="ffn",
        vmem=28,
    )


def view(ref, slot):
    return ref if slot is None else ref.at[slot]


def total_kernel(slots, low, *refs):
    out_ref = refs[-1]
    for piece in range(out_ref.shape[0]):
        total = None
        for slot, ref in zip(slots, refs[:-1]):
            term = view(ref, slot)[low + piece].astype(jnp.float32)
            total = term if total is None else total + term
        out_ref[piece] = total.astype(out_ref.dtype)


def total(terms, low, high):
    arrays = [a for a, _ in terms]
    shape = jax.ShapeDtypeStruct((high - low, *arrays[0].shape[-2:]), arrays[0].dtype)
    return call(
        functools.partial(total_kernel, [slot for _, slot in terms], low),
        arrays,
        [VMEM] * len(arrays),
        [shape],
        name="total",
    )[0]


def finish_kernel(slots, hidden_ref, *refs):
    out_ref = refs[-1]
    for batch in range(hidden_ref.shape[0]):
        mixed = None
        for i, slot in enumerate(slots):
            term = view(refs[batch * len(slots) + i], slot)[0].astype(jnp.float32)
            mixed = term if mixed is None else mixed + term
        out_ref[batch] = (hidden_ref[batch].astype(jnp.float32) + mixed).astype(out_ref.dtype)


def finish(hidden_in, terms):
    arrays = [a for batch in terms for a, _ in batch]
    return call(
        functools.partial(finish_kernel, [slot for _, slot in terms[0]]),
        [hidden_in, *arrays],
        [VMEM] * (1 + len(arrays)),
        [jax.ShapeDtypeStruct(hidden_in.shape, hidden_in.dtype)],
        name="finish",
        pin=False,
    )[0]


def local(
    hidden_in,
    expert_ids,
    route_share,
    norm_gain,
    gate_weight,
    up_weight,
    down_weight,
    exponent_table,
):
    owners = lax.axis_size("ep")
    batches = hidden_in.shape[0]
    weights = (gate_weight, up_weight, down_weight)
    scales = jnp.exp2(exponent_table[0].astype(jnp.float32))
    owner = lax.axis_index("ep").astype(jnp.int32).reshape(1)

    line = owners // 4
    half = line // 2

    def mirror(rows, span):
        def partner(i):
            p = i // 4
            return (p // span * span + span - 1 - p % span) * 4 + i % 4

        return lax.ppermute(rows, "ep", [(i, partner(i)) for i in range(owners)])

    def to_mid(rows):
        return lax.ppermute(rows, "ep", [(i, i ^ 2) for i in range(owners)])

    def to_core(rows):
        return lax.ppermute(rows, "ep", [(i, i ^ 1) for i in range(owners)])

    payload = prepare(hidden_in, expert_ids, route_share, norm_gain, -(-owners // LANES) * LANES)

    near, far = [], []
    for batch, rows in enumerate(payload):
        if batch:
            rows = after(rows, near[-1])
        span = line
        while span > 2:
            rows = join(rows, mirror(rows, span))
            if batch:
                rows = after(rows, far[-1])
            span //= 2
        near.append(rows)
        far.append(mirror(rows, 2))

    def expert(rows, there, *others):
        xs = [rows, there, to_core(rows), to_core(there)]
        mine, other = ffn([after(xs[0], *others), *xs[1:]], owner, scales, weights)
        other = to_core(other)
        sent.append(total([(mine, 1), (other, 1)], 0, half))
        back.append(to_mid(sent[-1]))
        return [(mine, 0), (other, 0), (back[-1], None)]

    near_terms, far_terms, sent, back = [], [], [], []
    near_there = [to_mid(rows) for rows in near]
    far_there = [to_mid(rows) for rows in far]
    for batch in range(batches):
        there = near_there[batch]
        if batch + 1 < batches:
            there = after(there, near[batch + 1])
        near_terms.append(expert(near[batch], there, far[-1], *sent[-1:], *back[-2:-1]))
        far_terms.append(expert(far[batch], far_there[batch], *sent[-1:], *back[-2:-1]))

    for batch in range(batches):
        terms = near_terms[batch]
        last = far_terms[batch]
        if batch + 1 < batches:
            last = [*last[:-1], (after(last[-1][0], sent[-1]), None)]
        terms.append((mirror(total(last, 0, half), 2), None))
        span, pieces = 4, half
        while pieces > 1:
            terms.append((mirror(total(terms, pieces // 2, pieces), span), None))
            span, pieces = span * 2, pieces // 2
    return finish(hidden_in, near_terms)


def solution(mesh):
    return jax.shard_map(
        local,
        mesh=mesh,
        in_specs=(
            P(None, ("grp", "ep"), None),
            P(None, ("grp", "ep"), None),
            P(None, ("grp", "ep"), None),
            P(),
            P("ep", None, None),
            P("ep", None, None),
            P("ep", None, None),
            P("ep", None, None),
        ),
        out_specs=P(None, ("grp", "ep"), None),
        check_vma=False,
    )
```

```python
import functools

import jax
import jax.numpy as jnp
from jax import lax
from jax.experimental import pallas as pl
from jax.experimental.pallas import tpu as pltpu
from jax.sharding import PartitionSpec as P

LANES = 128
VMEM = pl.BlockSpec(memory_space=pltpu.VMEM)
HBM = pl.BlockSpec(memory_space=pltpu.HBM)
SMEM = pl.BlockSpec(memory_space=pltpu.SMEM)
PINNED = {pltpu.VMEM, pltpu.HBM}


def call(kernel, operands, specs, shapes, scratch=(), name=None, vmem=8, pin=True):
    if pin:
        shapes = [pltpu.VMEM(s.shape, s.dtype) for s in shapes]
        operands = [
            pltpu.with_memory_space_constraint(a, spec.memory_space)
            if spec.memory_space in PINNED
            else a
            for a, spec in zip(operands, specs)
        ]
    return pl.pallas_call(
        kernel,
        out_shape=shapes,
        in_specs=specs,
        out_specs=[VMEM] * len(shapes),
        scratch_shapes=list(scratch),
        cost_estimate=pl.CostEstimate(flops=0, bytes_accessed=0, transcendentals=0),
        compiler_params=pltpu.CompilerParams(vmem_limit_bytes=vmem << 20),
        name=name,
    )(*operands)


def after(value, *others):
    return lax.optimization_barrier((value, *others))[0]


def prepare_kernel(hidden_hbm, ids_hbm, share_hbm, gain_hbm, *refs):
    out_refs, (hidden_ref, ids_ref, share_ref, gain_ref, sems) = refs[:-5], refs[-5:]
    sources = (hidden_hbm, ids_hbm, share_hbm, gain_hbm)
    targets = (hidden_ref, ids_ref, share_ref, gain_ref)
    copies = [pltpu.make_async_copy(s, t, sems.at[i]) for i, (s, t) in enumerate(zip(sources, targets))]
    for copy in copies:
        copy.start()
    for copy in copies:
        copy.wait()
    rows, width = hidden_ref.shape[1:]
    fanout = ids_ref.shape[1]
    extra = out_refs[0].shape[2] - width
    for batch, out_ref in enumerate(out_refs):
        values = hidden_ref[batch].astype(jnp.float32)
        power = jnp.mean(values * values, axis=-1, keepdims=True)
        normed = values * lax.rsqrt(power + 1e-06) * gain_ref[...]
        out_ref[0, :, :width] = normed.astype(jnp.bfloat16)
        expert = lax.broadcasted_iota(jnp.int32, (extra, rows), 0)
        dense = jnp.zeros((extra, rows), jnp.float32)
        for k in range(fanout):
            share = share_ref[batch, k : k + 1, :].astype(jnp.float32) * (1.0 / 64.0)
            dense = dense + jnp.where(expert == ids_ref[batch, k : k + 1, :], share, 0.0)
        out_ref[0, :, width:] = dense.T.astype(jnp.bfloat16)


def prepare(hidden_in, expert_ids, route_share, norm_gain, extra):
    batches, rows, width = hidden_in.shape
    operands = [
        hidden_in,
        expert_ids.transpose(0, 2, 1),
        route_share.transpose(0, 2, 1),
        norm_gain.reshape(1, width),
    ]
    return call(
        prepare_kernel,
        operands,
        [HBM] * 4,
        [jax.ShapeDtypeStruct((1, rows, width + extra), jnp.bfloat16)] * batches,
        [pltpu.VMEM(a.shape, a.dtype) for a in operands] + [pltpu.SemaphoreType.DMA((4,))],
        name="prepare",
    )


def join_kernel(*refs):
    at = 0
    for ref in refs[:-1]:
        refs[-1][at : at + ref.shape[0]] = ref[...]
        at += ref.shape[0]


def join(a, b):
    shape = jax.ShapeDtypeStruct((a.shape[0] + b.shape[0], *a.shape[1:]), a.dtype)
    return call(join_kernel, [a, b], [VMEM] * 2, [shape], name="join")[0]


def load_kernel(*refs):
    count = len(refs) // 2
    copies = [pltpu.make_async_copy(refs[i], refs[count + i], refs[-1].at[i]) for i in range(count)]
    for copy in copies:
        copy.start()
    for copy in copies:
        copy.wait()


def load(weights):
    return call(
        load_kernel,
        weights,
        [HBM] * len(weights),
        [jax.ShapeDtypeStruct(w.shape, w.dtype) for w in weights],
        [pltpu.SemaphoreType.DMA((len(weights),))],
        name="load",
    )


def ffn_kernel(owner_ref, scale_ref, gate_ref, up_ref, down_ref, *refs):
    x_refs, (mine_ref, other_ref, x_all, hidden) = refs[:-4], refs[-4:]
    width, ff = gate_ref.shape[1:]
    group = ff // scale_ref.shape[1]
    step = 2 * group if ff % (2 * group) == 0 else group
    _, pieces, part, _ = mine_ref.shape
    at = 0
    for x_ref in x_refs:
        rows = x_ref.shape[0] * part
        x_all[at : at + rows, :] = x_ref[...].reshape(rows, x_ref.shape[2])
        at += rows
    for f in range(0, ff, step):
        x = x_all[:, :width]
        gate = jnp.dot(x, gate_ref[0, :, f : f + step], preferred_element_type=jnp.float32)
        up = jnp.dot(x, up_ref[0, :, f : f + step], preferred_element_type=jnp.float32)
        for at in range(0, step, group):
            b = (f + at) // group
            g = gate[:, at : at + group] * scale_ref[0, b]
            u = up[:, at : at + group] * scale_ref[1, b]
            h = g / (1.0 + jnp.exp(-g)) * u * scale_ref[2, b]
            hidden[:, f + at : f + at + group] = h.astype(jnp.bfloat16)
    shares = x_all[:, width:].astype(jnp.float32)
    here = lax.broadcasted_iota(jnp.int32, shares.shape, 1) == owner_ref[0]
    weight = jnp.sum(jnp.where(here, shares, 0.0), axis=1, keepdims=True)
    cols = 512 if width % 512 == 0 else LANES
    for n in range(0, width, cols):
        out = jnp.dot(hidden[...], down_ref[0, :, n : n + cols], preferred_element_type=jnp.float32)
        out = (out * weight).astype(jnp.bfloat16).reshape(4, pieces, part, cols)
        mine_ref[:, :, :, n : n + cols] = out[:2]
        other_ref[:, :, :, n : n + cols] = out[2:]


def ffn(xs, owner, scales, weights):
    pieces = sum(x.shape[0] for x in xs) // 4
    _, part, full = xs[0].shape
    width, ff = weights[0].shape[1:]
    rows = 4 * pieces * part
    return call(
        ffn_kernel,
        [owner, scales, *weights, *xs],
        [SMEM, SMEM] + [VMEM] * (3 + len(xs)),
        [jax.ShapeDtypeStruct((2, pieces, part, width), jnp.bfloat16)] * 2,
        [pltpu.VMEM((rows, full), jnp.bfloat16), pltpu.VMEM((rows, ff), jnp.bfloat16)],
        name="ffn",
        vmem=16,
    )


def piece_of(ref, slot, piece):
    return ref[piece] if slot is None else ref[slot, piece]


def total_kernel(terms, low, *refs):
    out_ref = refs[-1]
    for piece in range(out_ref.shape[0]):
        total = None
        for (slot, first), ref in zip(terms, refs[:-1]):
            term = piece_of(ref, slot, low + piece - first).astype(jnp.float32)
            total = term if total is None else total + term
        out_ref[piece] = total.astype(out_ref.dtype)


def total(terms, low, high):
    arrays = [a for a, _, _ in terms]
    shape = jax.ShapeDtypeStruct((high - low, *arrays[0].shape[-2:]), arrays[0].dtype)
    return call(
        functools.partial(total_kernel, [where for _, *where in terms], low),
        arrays,
        [VMEM] * len(arrays),
        [shape],
        name="total",
    )[0]


def finish_kernel(terms, hidden_ref, *refs):
    out_ref = refs[-1]
    for batch in range(hidden_ref.shape[0]):
        mixed = None
        for i, (slot, first) in enumerate(terms):
            term = piece_of(refs[batch * len(terms) + i], slot, -first).astype(jnp.float32)
            mixed = term if mixed is None else mixed + term
        out_ref[batch] = (hidden_ref[batch].astype(jnp.float32) + mixed).astype(out_ref.dtype)


def finish(hidden_in, terms):
    arrays = [a for batch in terms for a, _, _ in batch]
    return call(
        functools.partial(finish_kernel, [where for _, *where in terms[0]]),
        [hidden_in, *arrays],
        [VMEM] * (1 + len(arrays)),
        [jax.ShapeDtypeStruct(hidden_in.shape, hidden_in.dtype)],
        name="finish",
        pin=False,
    )[0]


def local(
    hidden_in,
    expert_ids,
    route_share,
    norm_gain,
    gate_weight,
    up_weight,
    down_weight,
    exponent_table,
):
    owners = lax.axis_size("ep")
    batches = hidden_in.shape[0]
    weights = load([gate_weight, up_weight, down_weight])
    scales = jnp.exp2(exponent_table[0].astype(jnp.float32))
    owner = lax.axis_index("ep").astype(jnp.int32).reshape(1)

    line = owners // 4
    half = line // 2

    def mirror(rows, span):
        def partner(i):
            p = i // 4
            return (p // span * span + span - 1 - p % span) * 4 + i % 4

        return lax.ppermute(rows, "ep", [(i, partner(i)) for i in range(owners)])

    def to_mid(rows):
        return lax.ppermute(rows, "ep", [(i, i ^ 2) for i in range(owners)])

    def to_core(rows):
        return lax.ppermute(rows, "ep", [(i, i ^ 1) for i in range(owners)])

    payload = prepare(hidden_in, expert_ids, route_share, norm_gain, -(-owners // LANES) * LANES)

    near, far = [], []
    for batch, rows in enumerate(payload):
        if batch:
            rows = after(rows, near[-1])
        span = line
        while span > 2:
            received = mirror(rows, span)
            if not batch:
                received = after(received, *weights)
            rows = join(rows, received)
            if batch:
                rows = after(rows, far[-1])
            span //= 2
        near.append(rows)
        if not batch:
            near_there = to_mid(rows)
        far.append(mirror(rows if not batch else after(rows, near_there), 2))

    here, there = [], []
    for batch in range(batches):
        if batch == 0:
            here.append([near[0], far[0]])
            there.append([near_there, to_mid(far[0])])
        else:
            here.append([join(near[batch], far[batch])])
            there.append([to_mid(here[batch][0])])
    if batches > 1:
        there[0][0] = after(there[0][0], near[1])

    terms, sent, back = [], [], []
    for batch in range(batches):
        xs = here[batch] + there[batch] + [to_core(rows) for rows in here[batch] + there[batch]]
        xs[0] = after(xs[0], far[-1], *sent[-1:])
        mine, other = ffn(xs, owner, scales, weights)
        if batch + 1 < batches:
            other = after(other, *there[batch + 1])
        if batch:
            other = after(other, back[-1][0])
        other = to_core(other)
        own = [(mine, 1, 0), (other, 1, 0)]
        if batch + 1 < batches:
            sent.append(total(own, 0, line))
            back.append([to_mid(sent[-1])])
        else:
            sent.append(total(own, half, line))
            back.append([to_mid(total(own, 0, half)), to_mid(sent[-1])])
        terms.append([(mine, 0, 0), (other, 0, 0)])

    for batch in range(batches):
        near_back, far_back = back[batch][0], back[batch][-1]
        far_sum = total([*terms[batch], (far_back, None, line - far_back.shape[0])], half, line)
        terms[batch] += [(near_back, None, 0), (mirror(far_sum, 2), None, 0)]
        span, pieces = 4, half
        while pieces > 1:
            part = total(terms[batch], pieces // 2, pieces)
            terms[batch].append((mirror(part, span), None, 0))
            span, pieces = span * 2, pieces // 2
    return finish(hidden_in, terms)


def solution(mesh):
    return jax.shard_map(
        local,
        mesh=mesh,
        in_specs=(
            P(None, ("grp", "ep"), None),
            P(None, ("grp", "ep"), None),
            P(None, ("grp", "ep"), None),
            P(),
            P("ep", None, None),
            P("ep", None, None),
            P("ep", None, None),
            P("ep", None, None),
        ),
        out_specs=P(None, ("grp", "ep"), None),
        check_vma=False,
    )
```

```python
import functools

import jax
import jax.numpy as jnp
from jax import lax
from jax.experimental import pallas as pl
from jax.experimental.pallas import tpu as pltpu
from jax.sharding import PartitionSpec as P

LANES = 128
VMEM = pl.BlockSpec(memory_space=pltpu.VMEM)
HBM = pl.BlockSpec(memory_space=pltpu.HBM)
SMEM = pl.BlockSpec(memory_space=pltpu.SMEM)
PINNED = {pltpu.VMEM, pltpu.HBM}


def call(kernel, operands, specs, shapes, scratch=(), name=None, vmem=8, pin=True):
    if pin:
        shapes = [pltpu.VMEM(s.shape, s.dtype) for s in shapes]
        operands = [
            pltpu.with_memory_space_constraint(a, spec.memory_space)
            if spec.memory_space in PINNED
            else a
            for a, spec in zip(operands, specs)
        ]
    return pl.pallas_call(
        kernel,
        out_shape=shapes,
        in_specs=specs,
        out_specs=[VMEM] * len(shapes),
        scratch_shapes=list(scratch),
        cost_estimate=pl.CostEstimate(flops=0, bytes_accessed=0, transcendentals=0),
        compiler_params=pltpu.CompilerParams(vmem_limit_bytes=vmem << 20),
        name=name,
    )(*operands)


def after(value, *others):
    return lax.optimization_barrier((value, *others))[0]


def prepare_kernel(hidden_hbm, ids_hbm, share_hbm, gain_hbm, *refs):
    out_refs, (hidden_ref, ids_ref, share_ref, gain_ref, sems) = refs[:-5], refs[-5:]
    sources = (hidden_hbm, ids_hbm, share_hbm, gain_hbm)
    targets = (hidden_ref, ids_ref, share_ref, gain_ref)
    copies = [pltpu.make_async_copy(s, t, sems.at[i]) for i, (s, t) in enumerate(zip(sources, targets))]
    for copy in copies:
        copy.start()
    for copy in copies:
        copy.wait()
    rows, width = hidden_ref.shape[1:]
    fanout = ids_ref.shape[1]
    extra = out_refs[0].shape[2] - width
    for batch, out_ref in enumerate(out_refs):
        values = hidden_ref[batch].astype(jnp.float32)
        power = jnp.mean(values * values, axis=-1, keepdims=True)
        normed = values * lax.rsqrt(power + 1e-06) * gain_ref[...]
        out_ref[0, :, :width] = normed.astype(jnp.bfloat16)
        expert = lax.broadcasted_iota(jnp.int32, (extra, rows), 0)
        dense = jnp.zeros((extra, rows), jnp.float32)
        for k in range(fanout):
            share = share_ref[batch, k : k + 1, :].astype(jnp.float32) * (1.0 / 64.0)
            dense = dense + jnp.where(expert == ids_ref[batch, k : k + 1, :], share, 0.0)
        out_ref[0, :, width:] = dense.T.astype(jnp.bfloat16)


def prepare(hidden_in, expert_ids, route_share, norm_gain, extra):
    batches, rows, width = hidden_in.shape
    operands = [
        hidden_in,
        expert_ids.transpose(0, 2, 1),
        route_share.transpose(0, 2, 1),
        norm_gain.reshape(1, width),
    ]
    return call(
        prepare_kernel,
        operands,
        [HBM] * 4,
        [jax.ShapeDtypeStruct((1, rows, width + extra), jnp.bfloat16)] * batches,
        [pltpu.VMEM(a.shape, a.dtype) for a in operands] + [pltpu.SemaphoreType.DMA((4,))],
        name="prepare",
    )


def join_kernel(*refs):
    at = 0
    for ref in refs[:-1]:
        refs[-1][at : at + ref.shape[0]] = ref[...]
        at += ref.shape[0]


def join(a, b):
    shape = jax.ShapeDtypeStruct((a.shape[0] + b.shape[0], *a.shape[1:]), a.dtype)
    return call(join_kernel, [a, b], [VMEM] * 2, [shape], name="join")[0]


def load_kernel(*refs):
    count = len(refs) // 2
    copies = [pltpu.make_async_copy(refs[i], refs[count + i], refs[-1].at[i]) for i in range(count)]
    for copy in copies:
        copy.start()
    for copy in copies:
        copy.wait()


def load(weights):
    return call(
        load_kernel,
        weights,
        [HBM] * len(weights),
        [jax.ShapeDtypeStruct(w.shape, w.dtype) for w in weights],
        [pltpu.SemaphoreType.DMA((len(weights),))],
        name="load",
    )


def ffn_kernel(owner_ref, scale_ref, gate_ref, up_ref, down_ref, *refs):
    x_refs, (mine_ref, other_ref, x_all, hidden) = refs[:-4], refs[-4:]
    width, ff = gate_ref.shape[1:]
    group = ff // scale_ref.shape[1]
    step = 2 * group if ff % (2 * group) == 0 else group
    _, pieces, part, _ = mine_ref.shape
    at = 0
    for x_ref in x_refs:
        rows = x_ref.shape[0] * part
        x_all[at : at + rows, :] = x_ref[...].reshape(rows, x_ref.shape[2])
        at += rows
    for f in range(0, ff, step):
        x = x_all[:, :width]
        gate = jnp.dot(x, gate_ref[0, :, f : f + step], preferred_element_type=jnp.float32)
        up = jnp.dot(x, up_ref[0, :, f : f + step], preferred_element_type=jnp.float32)
        for at in range(0, step, group):
            b = (f + at) // group
            g = gate[:, at : at + group] * scale_ref[0, b]
            u = up[:, at : at + group] * scale_ref[1, b]
            h = g / (1.0 + jnp.exp(-g)) * u * scale_ref[2, b]
            hidden[:, f + at : f + at + group] = h.astype(jnp.bfloat16)
    shares = x_all[:, width:].astype(jnp.float32)
    here = lax.broadcasted_iota(jnp.int32, shares.shape, 1) == owner_ref[0]
    weight = jnp.sum(jnp.where(here, shares, 0.0), axis=1, keepdims=True)
    cols = 512 if width % 512 == 0 else LANES
    for n in range(0, width, cols):
        out = jnp.dot(hidden[...], down_ref[0, :, n : n + cols], preferred_element_type=jnp.float32)
        out = (out * weight).astype(jnp.bfloat16).reshape(4, pieces, part, cols)
        mine_ref[:, :, :, n : n + cols] = out[:2]
        other_ref[:, :, :, n : n + cols] = out[2:]


def ffn(xs, owner, scales, weights):
    pieces = sum(x.shape[0] for x in xs) // 4
    _, part, full = xs[0].shape
    width, ff = weights[0].shape[1:]
    rows = 4 * pieces * part
    return call(
        ffn_kernel,
        [owner, scales, *weights, *xs],
        [SMEM, SMEM] + [VMEM] * (3 + len(xs)),
        [jax.ShapeDtypeStruct((2, pieces, part, width), jnp.bfloat16)] * 2,
        [pltpu.VMEM((rows, full), jnp.bfloat16), pltpu.VMEM((rows, ff), jnp.bfloat16)],
        name="ffn",
        vmem=16,
    )


def piece_of(ref, slot, piece):
    return ref[piece] if slot is None else ref[slot, piece]


def total_kernel(terms, low, *refs):
    out_ref = refs[-1]
    for piece in range(out_ref.shape[0]):
        total = None
        for (slot, first), ref in zip(terms, refs[:-1]):
            term = piece_of(ref, slot, low + piece - first).astype(jnp.float32)
            total = term if total is None else total + term
        out_ref[piece] = total.astype(out_ref.dtype)


def total(terms, low, high):
    arrays = [a for a, _, _ in terms]
    shape = jax.ShapeDtypeStruct((high - low, *arrays[0].shape[-2:]), arrays[0].dtype)
    return call(
        functools.partial(total_kernel, [where for _, *where in terms], low),
        arrays,
        [VMEM] * len(arrays),
        [shape],
        name="total",
    )[0]


def finish_kernel(terms, hidden_ref, *refs):
    out_ref = refs[-1]
    for batch in range(hidden_ref.shape[0]):
        mixed = None
        for i, (slot, first) in enumerate(terms):
            term = piece_of(refs[batch * len(terms) + i], slot, -first).astype(jnp.float32)
            mixed = term if mixed is None else mixed + term
        out_ref[batch] = (hidden_ref[batch].astype(jnp.float32) + mixed).astype(out_ref.dtype)


def finish(hidden_in, terms):
    arrays = [a for batch in terms for a, _, _ in batch]
    return call(
        functools.partial(finish_kernel, [where for _, *where in terms[0]]),
        [hidden_in, *arrays],
        [VMEM] * (1 + len(arrays)),
        [jax.ShapeDtypeStruct(hidden_in.shape, hidden_in.dtype)],
        name="finish",
        pin=False,
    )[0]


def local(
    hidden_in,
    expert_ids,
    route_share,
    norm_gain,
    gate_weight,
    up_weight,
    down_weight,
    exponent_table,
):
    owners = lax.axis_size("ep")
    batches = hidden_in.shape[0]
    scales = jnp.exp2(exponent_table[0].astype(jnp.float32))
    owner = lax.axis_index("ep").astype(jnp.int32).reshape(1)

    line = owners // 4
    half = line // 2

    def mirror(rows, span):
        def partner(i):
            p = i // 4
            return (p // span * span + span - 1 - p % span) * 4 + i % 4

        return lax.ppermute(rows, "ep", [(i, partner(i)) for i in range(owners)])

    def to_mid(rows):
        return lax.ppermute(rows, "ep", [(i, i ^ 2) for i in range(owners)])

    def to_core(rows):
        return lax.ppermute(rows, "ep", [(i, i ^ 1) for i in range(owners)])

    payload = prepare(hidden_in, expert_ids, route_share, norm_gain, -(-owners // LANES) * LANES)

    own_there = [to_mid(rows) for rows in payload]
    near, far, there = [], [], []
    for batch, rows in enumerate(payload):
        if batch:
            rows = after(rows, near[-1])
        there.append([own_there[batch]])
        span = line
        while span > 2:
            received = mirror(rows, span)
            if not batch:
                received = after(received, *own_there)
            there[batch].append(to_mid(received))
            rows = join(rows, received)
            if batch:
                rows = after(rows, far[-1])
            span //= 2
        near.append(rows)
        far.append(mirror(rows if not batch else after(rows, *there[batch - 1]), 2))
    weights = load([after(w, near[-1]) for w in (gate_weight, up_weight, down_weight)])
    far[-1] = after(far[-1], *weights)
    ahead = there[-1][-1]
    for batch in range(batches):
        rows = far[batch]
        if batch + 1 < batches:
            rows = after(rows, near[batch + 1])
        there[batch].append(to_mid(rows))

    terms, sent, back = [], [], []
    for batch in range(batches):
        xs = [near[batch], far[batch], *there[batch]]
        xs += [to_core(rows) for rows in xs]
        xs[0] = after(xs[0], far[-1], ahead, *sent[-1:])
        mine, other = ffn(xs, owner, scales, weights)
        if batch + 1 < batches:
            other = after(other, *there[batch + 1])
        if batch:
            other = after(other, back[-1][0])
        other = to_core(other)
        own = [(mine, 1, 0), (other, 1, 0)]
        if batch + 1 < batches:
            sent.append(total(own, 0, line))
            back.append([to_mid(sent[-1])])
        else:
            sent.append(total(own, half, line))
            back.append([to_mid(total(own, 0, half)), to_mid(sent[-1])])
        terms.append([(mine, 0, 0), (other, 0, 0)])

    for batch in range(batches):
        near_back, far_back = back[batch][0], back[batch][-1]
        far_sum = total([*terms[batch], (far_back, None, line - far_back.shape[0])], half, line)
        terms[batch] += [(near_back, None, 0), (mirror(far_sum, 2), None, 0)]
        span, pieces = 4, half
        while pieces > 1:
            part = total(terms[batch], pieces // 2, pieces)
            terms[batch].append((mirror(part, span), None, 0))
            span, pieces = span * 2, pieces // 2
    return finish(hidden_in, terms)


def solution(mesh):
    return jax.shard_map(
        local,
        mesh=mesh,
        in_specs=(
            P(None, ("grp", "ep"), None),
            P(None, ("grp", "ep"), None),
            P(None, ("grp", "ep"), None),
            P(),
            P("ep", None, None),
            P("ep", None, None),
            P("ep", None, None),
            P("ep", None, None),
        ),
        out_specs=P(None, ("grp", "ep"), None),
        check_vma=False,
    )
```

```python
import functools

import jax
import jax.numpy as jnp
from jax import lax
from jax.experimental import pallas as pl
from jax.experimental.pallas import tpu as pltpu
from jax.sharding import PartitionSpec as P

LANES = 128
VMEM = pl.BlockSpec(memory_space=pltpu.VMEM)
HBM = pl.BlockSpec(memory_space=pltpu.HBM)
SMEM = pl.BlockSpec(memory_space=pltpu.SMEM)
PINNED = {pltpu.VMEM, pltpu.HBM}


def call(kernel, operands, specs, shapes, scratch=(), name=None, vmem=8, pin=True):
    if pin:
        shapes = [pltpu.VMEM(s.shape, s.dtype) for s in shapes]
        operands = [
            pltpu.with_memory_space_constraint(a, spec.memory_space)
            if spec.memory_space in PINNED
            else a
            for a, spec in zip(operands, specs)
        ]
    return pl.pallas_call(
        kernel,
        out_shape=shapes,
        in_specs=specs,
        out_specs=[VMEM] * len(shapes),
        scratch_shapes=list(scratch),
        cost_estimate=pl.CostEstimate(flops=0, bytes_accessed=0, transcendentals=0),
        compiler_params=pltpu.CompilerParams(vmem_limit_bytes=vmem << 20),
        name=name,
    )(*operands)


def after(value, *others):
    return lax.optimization_barrier((value, *others))[0]


def prepare_kernel(hidden_hbm, ids_hbm, share_hbm, gain_hbm, *refs):
    out_refs, (hidden_ref, ids_ref, share_ref, gain_ref, sems) = refs[:-5], refs[-5:]
    sources = (hidden_hbm, ids_hbm, share_hbm, gain_hbm)
    targets = (hidden_ref, ids_ref, share_ref, gain_ref)
    copies = [pltpu.make_async_copy(s, t, sems.at[i]) for i, (s, t) in enumerate(zip(sources, targets))]
    for copy in copies:
        copy.start()
    for copy in copies:
        copy.wait()
    rows, width = hidden_ref.shape[1:]
    fanout = ids_ref.shape[1]
    extra = out_refs[0].shape[2] - width
    for batch, out_ref in enumerate(out_refs):
        values = hidden_ref[batch].astype(jnp.float32)
        power = jnp.mean(values * values, axis=-1, keepdims=True)
        normed = values * lax.rsqrt(power + 1e-06) * gain_ref[...]
        out_ref[0, :, :width] = normed.astype(jnp.bfloat16)
        expert = lax.broadcasted_iota(jnp.int32, (extra, rows), 0)
        dense = jnp.zeros((extra, rows), jnp.float32)
        for k in range(fanout):
            share = share_ref[batch, k : k + 1, :].astype(jnp.float32) * (1.0 / 64.0)
            dense = dense + jnp.where(expert == ids_ref[batch, k : k + 1, :], share, 0.0)
        out_ref[0, :, width:] = dense.T.astype(jnp.bfloat16)


def prepare(hidden_in, expert_ids, route_share, norm_gain, extra):
    batches, rows, width = hidden_in.shape
    operands = [
        hidden_in,
        expert_ids.transpose(0, 2, 1),
        route_share.transpose(0, 2, 1),
        norm_gain.reshape(1, width),
    ]
    return call(
        prepare_kernel,
        operands,
        [HBM] * 4,
        [jax.ShapeDtypeStruct((1, rows, width + extra), jnp.bfloat16)] * batches,
        [pltpu.VMEM(a.shape, a.dtype) for a in operands] + [pltpu.SemaphoreType.DMA((4,))],
        name="prepare",
    )


def join_kernel(*refs):
    at = 0
    for ref in refs[:-1]:
        refs[-1][at : at + ref.shape[0]] = ref[...]
        at += ref.shape[0]


def join(a, b):
    shape = jax.ShapeDtypeStruct((a.shape[0] + b.shape[0], *a.shape[1:]), a.dtype)
    return call(join_kernel, [a, b], [VMEM] * 2, [shape], name="join")[0]


def load_kernel(*refs):
    count = len(refs) // 2
    copies = [pltpu.make_async_copy(refs[i], refs[count + i], refs[-1].at[i]) for i in range(count)]
    for copy in copies:
        copy.start()
    for copy in copies:
        copy.wait()


def load(weights):
    return call(
        load_kernel,
        weights,
        [HBM] * len(weights),
        [jax.ShapeDtypeStruct(w.shape, w.dtype) for w in weights],
        [pltpu.SemaphoreType.DMA((len(weights),))],
        name="load",
    )


def ffn_kernel(table_ref, gate_ref, up_ref, down_ref, *refs):
    x_refs, (mine_ref, other_ref, x_all, hidden) = refs[:-4], refs[-4:]
    width, ff = gate_ref.shape[1:]
    group = ff // table_ref.shape[2]
    step = 2 * group if ff % (2 * group) == 0 else group
    _, pieces, part, _ = mine_ref.shape
    at = 0
    for x_ref in x_refs:
        rows = x_ref.shape[0] * part
        x_all[at : at + rows, :] = x_ref[...].reshape(rows, x_ref.shape[2])
        at += rows

    def scale(which, b):
        return jnp.exp2(jnp.full((1, group), table_ref[which, 0, b], jnp.int32).astype(jnp.float32))

    for f in range(0, ff, step):
        x = x_all[:, :width]
        gate = jnp.dot(x, gate_ref[0, :, f : f + step], preferred_element_type=jnp.float32)
        up = jnp.dot(x, up_ref[0, :, f : f + step], preferred_element_type=jnp.float32)
        for at in range(0, step, group):
            b = (f + at) // group
            g = gate[:, at : at + group] * scale(0, b)
            u = up[:, at : at + group] * scale(1, b)
            h = g / (1.0 + jnp.exp(-g)) * u * scale(2, b)
            hidden[:, f + at : f + at + group] = h.astype(jnp.bfloat16)
    shares = x_all[:, width:].astype(jnp.float32)
    here = lax.broadcasted_iota(jnp.int32, shares.shape, 1) == lax.axis_index("ep")
    weight = jnp.sum(jnp.where(here, shares, 0.0), axis=1, keepdims=True)
    cols = 512 if width % 512 == 0 else LANES
    for n in range(0, width, cols):
        out = jnp.dot(hidden[...], down_ref[0, :, n : n + cols], preferred_element_type=jnp.float32)
        out = (out * weight).astype(jnp.bfloat16).reshape(4, pieces, part, cols)
        mine_ref[:, :, :, n : n + cols] = out[:2]
        other_ref[:, :, :, n : n + cols] = out[2:]


def ffn(xs, table, weights):
    pieces = sum(x.shape[0] for x in xs) // 4
    _, part, full = xs[0].shape
    width, ff = weights[0].shape[1:]
    rows = 4 * pieces * part
    return call(
        ffn_kernel,
        [table, *weights, *xs],
        [SMEM] + [VMEM] * (3 + len(xs)),
        [jax.ShapeDtypeStruct((2, pieces, part, width), jnp.bfloat16)] * 2,
        [pltpu.VMEM((rows, full), jnp.bfloat16), pltpu.VMEM((rows, ff), jnp.bfloat16)],
        name="ffn",
        vmem=16,
    )


def piece_of(ref, slot, piece):
    return ref[piece] if slot is None else ref[slot, piece]


def total_kernel(terms, low, *refs):
    out_ref = refs[-1]
    for piece in range(out_ref.shape[0]):
        total = None
        for (slot, first), ref in zip(terms, refs[:-1]):
            term = piece_of(ref, slot, low + piece - first).astype(jnp.float32)
            total = term if total is None else total + term
        out_ref[piece] = total.astype(out_ref.dtype)


def total(terms, low, high):
    arrays = [a for a, _, _ in terms]
    shape = jax.ShapeDtypeStruct((high - low, *arrays[0].shape[-2:]), arrays[0].dtype)
    return call(
        functools.partial(total_kernel, [where for _, *where in terms], low),
        arrays,
        [VMEM] * len(arrays),
        [shape],
        name="total",
    )[0]


def finish_kernel(terms, hidden_ref, *refs):
    out_ref = refs[-1]
    for batch in range(hidden_ref.shape[0]):
        mixed = None
        for i, (slot, first) in enumerate(terms):
            term = piece_of(refs[batch * len(terms) + i], slot, -first).astype(jnp.float32)
            mixed = term if mixed is None else mixed + term
        out_ref[batch] = (hidden_ref[batch].astype(jnp.float32) + mixed).astype(out_ref.dtype)


def finish(hidden_in, terms):
    arrays = [a for batch in terms for a, _, _ in batch]
    return call(
        functools.partial(finish_kernel, [where for _, *where in terms[0]]),
        [hidden_in, *arrays],
        [VMEM] * (1 + len(arrays)),
        [jax.ShapeDtypeStruct(hidden_in.shape, hidden_in.dtype)],
        name="finish",
        pin=False,
    )[0]


def local(
    hidden_in,
    expert_ids,
    route_share,
    norm_gain,
    gate_weight,
    up_weight,
    down_weight,
    exponent_table,
):
    owners = lax.axis_size("ep")
    batches = hidden_in.shape[0]
    table = exponent_table.transpose(1, 0, 2)

    line = owners // 4
    half = line // 2

    def mirror(rows, span):
        def partner(i):
            p = i // 4
            return (p // span * span + span - 1 - p % span) * 4 + i % 4

        return lax.ppermute(rows, "ep", [(i, partner(i)) for i in range(owners)])

    def to_mid(rows):
        return lax.ppermute(rows, "ep", [(i, i ^ 2) for i in range(owners)])

    def to_core(rows):
        return lax.ppermute(rows, "ep", [(i, i ^ 1) for i in range(owners)])

    payload = prepare(hidden_in, expert_ids, route_share, norm_gain, -(-owners // LANES) * LANES)

    own_there = [to_mid(rows) for rows in payload]
    near, far, there = [], [], []
    for batch, rows in enumerate(payload):
        if batch:
            rows = after(rows, near[-1])
        there.append([own_there[batch]])
        span = line
        while span > 2:
            received = mirror(rows, span)
            if not batch:
                received = after(received, *own_there)
            there[batch].append(to_mid(received))
            rows = join(rows, received)
            if batch:
                rows = after(rows, far[-1])
            span //= 2
        near.append(rows)
        far.append(mirror(rows if not batch else after(rows, *there[batch - 1]), 2))
    weights = load([after(w, near[-1]) for w in (gate_weight, up_weight, down_weight)])
    far[-1] = after(far[-1], *weights)
    ahead = there[-1][-1]
    for batch in range(batches):
        rows = far[batch]
        if batch + 1 < batches:
            rows = after(rows, near[batch + 1])
        there[batch].append(to_mid(rows))

    terms, sent, back = [], [], []
    for batch in range(batches):
        xs = [near[batch], far[batch], *there[batch]]
        xs += [to_core(rows) for rows in xs]
        xs[0] = after(xs[0], far[-1], ahead, *sent[-1:])
        mine, other = ffn(xs, table, weights)
        if batch + 1 < batches:
            other = after(other, *there[batch + 1])
        if batch:
            other = after(other, back[-1][0])
        other = to_core(other)
        own = [(mine, 1, 0), (other, 1, 0)]
        if batch + 1 < batches:
            sent.append(total(own, 0, line))
            back.append([to_mid(sent[-1])])
        else:
            sent.append(total(own, half, line))
            back.append([to_mid(total(own, 0, half)), to_mid(sent[-1])])
        terms.append([(mine, 0, 0), (other, 0, 0)])

    for batch in range(batches):
        near_back, far_back = back[batch][0], back[batch][-1]
        far_sum = total([*terms[batch], (far_back, None, line - far_back.shape[0])], half, line)
        terms[batch] += [(near_back, None, 0), (mirror(far_sum, 2), None, 0)]
        span, pieces = 4, half
        while pieces > 1:
            part = total(terms[batch], pieces // 2, pieces)
            terms[batch].append((mirror(part, span), None, 0))
            span, pieces = span * 2, pieces // 2
    return finish(hidden_in, terms)


def solution(mesh):
    return jax.shard_map(
        local,
        mesh=mesh,
        in_specs=(
            P(None, ("grp", "ep"), None),
            P(None, ("grp", "ep"), None),
            P(None, ("grp", "ep"), None),
            P(),
            P("ep", None, None),
            P("ep", None, None),
            P("ep", None, None),
            P("ep", None, None),
        ),
        out_specs=P(None, ("grp", "ep"), None),
        check_vma=False,
    )
```

```python
import functools

import jax
import jax.numpy as jnp
from jax import lax
from jax.experimental import pallas as pl
from jax.experimental.pallas import tpu as pltpu
from jax.sharding import PartitionSpec as P

LANES = 128
VMEM = pl.BlockSpec(memory_space=pltpu.VMEM)
HBM = pl.BlockSpec(memory_space=pltpu.HBM)
SMEM = pl.BlockSpec(memory_space=pltpu.SMEM)
PINNED = {pltpu.VMEM, pltpu.HBM}


def call(kernel, operands, specs, shapes, scratch=(), name=None, vmem=8, pin=True):
    if pin:
        shapes = [pltpu.VMEM(s.shape, s.dtype) for s in shapes]
        operands = [
            pltpu.with_memory_space_constraint(a, spec.memory_space)
            if spec.memory_space in PINNED
            else a
            for a, spec in zip(operands, specs)
        ]
    return pl.pallas_call(
        kernel,
        out_shape=shapes,
        in_specs=specs,
        out_specs=[VMEM] * len(shapes),
        scratch_shapes=list(scratch),
        cost_estimate=pl.CostEstimate(flops=0, bytes_accessed=0, transcendentals=0),
        compiler_params=pltpu.CompilerParams(vmem_limit_bytes=vmem << 20),
        name=name,
    )(*operands)


def after(value, *others):
    return lax.optimization_barrier((value, *others))[0]


def prepare_kernel(hidden_hbm, ids_hbm, share_hbm, gain_hbm, *refs):
    out_refs, (hidden_ref, ids_ref, share_ref, gain_ref, sems) = refs[:-5], refs[-5:]
    sources = (hidden_hbm, ids_hbm, share_hbm, gain_hbm)
    targets = (hidden_ref, ids_ref, share_ref, gain_ref)
    copies = [pltpu.make_async_copy(s, t, sems.at[i]) for i, (s, t) in enumerate(zip(sources, targets))]
    for copy in copies:
        copy.start()
    for copy in copies:
        copy.wait()
    rows, width = hidden_ref.shape[1:]
    fanout = ids_ref.shape[1]
    extra = out_refs[0].shape[2] - width
    for batch, out_ref in enumerate(out_refs):
        values = hidden_ref[batch].astype(jnp.float32)
        power = jnp.mean(values * values, axis=-1, keepdims=True)
        normed = values * lax.rsqrt(power + 1e-06) * gain_ref[...]
        out_ref[0, :, :width] = normed.astype(jnp.bfloat16)
        expert = lax.broadcasted_iota(jnp.int32, (extra, rows), 0)
        dense = jnp.zeros((extra, rows), jnp.float32)
        for k in range(fanout):
            share = share_ref[batch, k : k + 1, :].astype(jnp.float32) * (1.0 / 64.0)
            dense = dense + jnp.where(expert == ids_ref[batch, k : k + 1, :], share, 0.0)
        out_ref[0, :, width:] = dense.T.astype(jnp.bfloat16)


def prepare(hidden_in, expert_ids, route_share, norm_gain, extra):
    batches, rows, width = hidden_in.shape
    operands = [
        hidden_in,
        expert_ids.transpose(0, 2, 1),
        route_share.transpose(0, 2, 1),
        norm_gain.reshape(1, width),
    ]
    return call(
        prepare_kernel,
        operands,
        [HBM] * 4,
        [jax.ShapeDtypeStruct((1, rows, width + extra), jnp.bfloat16)] * batches,
        [pltpu.VMEM(a.shape, a.dtype) for a in operands] + [pltpu.SemaphoreType.DMA((4,))],
        name="prepare",
    )


def join_kernel(*refs):
    at = 0
    for ref in refs[:-1]:
        refs[-1][at : at + ref.shape[0]] = ref[...]
        at += ref.shape[0]


def join(a, b):
    shape = jax.ShapeDtypeStruct((a.shape[0] + b.shape[0], *a.shape[1:]), a.dtype)
    return call(join_kernel, [a, b], [VMEM] * 2, [shape], name="join")[0]


def load_kernel(*refs):
    count = len(refs) // 2
    copies = [pltpu.make_async_copy(refs[i], refs[count + i], refs[-1].at[i]) for i in range(count)]
    for copy in copies:
        copy.start()
    for copy in copies:
        copy.wait()


def load(weights):
    return call(
        load_kernel,
        weights,
        [HBM] * len(weights),
        [jax.ShapeDtypeStruct(w.shape, w.dtype) for w in weights],
        [pltpu.SemaphoreType.DMA((len(weights),))],
        name="load",
    )


def ffn_kernel(table_ref, gate_ref, up_ref, down_ref, *refs):
    x_refs, (mine_ref, other_ref, x_all, hidden) = refs[:-4], refs[-4:]
    width, ff = gate_ref.shape[1:]
    group = ff // table_ref.shape[2]
    step = 2 * group if ff % (2 * group) == 0 else group
    _, pieces, part, _ = mine_ref.shape
    at = 0
    for x_ref in x_refs:
        rows = x_ref.shape[0] * part
        x_all[at : at + rows, :] = x_ref[...].reshape(rows, x_ref.shape[2])
        at += rows

    def scale(which, b):
        return jnp.exp2(jnp.full((1, group), table_ref[which, 0, b], jnp.int32).astype(jnp.float32))

    for f in range(0, ff, step):
        x = x_all[:, :width]
        gate = jnp.dot(x, gate_ref[0, :, f : f + step], preferred_element_type=jnp.float32)
        up = jnp.dot(x, up_ref[0, :, f : f + step], preferred_element_type=jnp.float32)
        for at in range(0, step, group):
            b = (f + at) // group
            g = gate[:, at : at + group] * scale(0, b)
            u = up[:, at : at + group] * scale(1, b)
            h = g / (1.0 + jnp.exp(-g)) * u * scale(2, b)
            hidden[:, f + at : f + at + group] = h.astype(jnp.bfloat16)
    shares = x_all[:, width:].astype(jnp.float32)
    here = lax.broadcasted_iota(jnp.int32, shares.shape, 1) == lax.axis_index("ep")
    weight = jnp.sum(jnp.where(here, shares, 0.0), axis=1, keepdims=True)
    cols = 512 if width % 512 == 0 else LANES
    for n in range(0, width, cols):
        out = jnp.dot(hidden[...], down_ref[0, :, n : n + cols], preferred_element_type=jnp.float32)
        out = (out * weight).astype(jnp.bfloat16).reshape(4, pieces, part, cols)
        mine_ref[:, :, :, n : n + cols] = out[:2]
        other_ref[:, :, :, n : n + cols] = out[2:]


def ffn(xs, table, weights):
    pieces = sum(x.shape[0] for x in xs) // 4
    _, part, full = xs[0].shape
    width, ff = weights[0].shape[1:]
    rows = 4 * pieces * part
    return call(
        ffn_kernel,
        [table, *weights, *xs],
        [SMEM] + [VMEM] * (3 + len(xs)),
        [jax.ShapeDtypeStruct((2, pieces, part, width), jnp.bfloat16)] * 2,
        [pltpu.VMEM((rows, full), jnp.bfloat16), pltpu.VMEM((rows, ff), jnp.bfloat16)],
        name="ffn",
        vmem=16,
    )


def piece_of(ref, slot, piece):
    return ref[piece] if slot is None else ref[slot, piece]


def total_kernel(terms, cuts, *refs):
    ins, outs = refs[: len(terms)], refs[len(terms) :]
    for (low, high), out_ref in zip(cuts, outs):
        for piece in range(low, high):
            total = None
            for (slot, first), ref in zip(terms, ins):
                term = piece_of(ref, slot, piece - first).astype(jnp.float32)
                total = term if total is None else total + term
            out_ref[piece - low] = total.astype(out_ref.dtype)


def total(terms, cuts):
    arrays = [a for a, _, _ in terms]
    _, _, part, width = arrays[0].shape
    shapes = [jax.ShapeDtypeStruct((high - low, part, width), arrays[0].dtype) for low, high in cuts]
    return call(
        functools.partial(total_kernel, [where for _, *where in terms], cuts),
        arrays,
        [VMEM] * len(arrays),
        shapes,
        name="total",
    )


def finish_kernel(terms, hidden_ref, *refs):
    out_ref = refs[-1]
    for batch in range(hidden_ref.shape[0]):
        mixed = None
        for i, (slot, first) in enumerate(terms):
            term = piece_of(refs[batch * len(terms) + i], slot, -first).astype(jnp.float32)
            mixed = term if mixed is None else mixed + term
        out_ref[batch] = (hidden_ref[batch].astype(jnp.float32) + mixed).astype(out_ref.dtype)


def finish(hidden_in, terms):
    arrays = [a for batch in terms for a, _, _ in batch]
    return call(
        functools.partial(finish_kernel, [where for _, *where in terms[0]]),
        [hidden_in, *arrays],
        [VMEM] * (1 + len(arrays)),
        [jax.ShapeDtypeStruct(hidden_in.shape, hidden_in.dtype)],
        name="finish",
        pin=False,
    )[0]


def local(
    hidden_in,
    expert_ids,
    route_share,
    norm_gain,
    gate_weight,
    up_weight,
    down_weight,
    exponent_table,
):
    owners = lax.axis_size("ep")
    batches = hidden_in.shape[0]
    table = exponent_table.transpose(1, 0, 2)

    line = owners // 4
    half = line // 2

    def along_line(rows, place_of):
        return lax.ppermute(rows, "ep", [(i, place_of(i // 4) * 4 + i % 4) for i in range(owners)])

    def mirrored(p, span):
        return p // span * span + span - 1 - p % span

    def mirror(rows, span):
        return along_line(rows, lambda p: mirrored(p, span))

    def to_mid(rows):
        return lax.ppermute(rows, "ep", [(i, i ^ 2) for i in range(owners)])

    def to_core(rows):
        return lax.ppermute(rows, "ep", [(i, i ^ 1) for i in range(owners)])

    spans = []
    while line >> len(spans) > 2:
        spans.append(line >> len(spans))

    def owner_of(p, piece, levels):
        for level in range(levels, 0, -1):
            if piece >= 1 << (level - 1):
                p, piece = mirrored(p, spans[level - 1]), piece - (1 << (level - 1))
        return p

    payload = prepare(hidden_in, expert_ids, route_share, norm_gain, -(-owners // LANES) * LANES)

    own_there = [to_mid(rows) for rows in payload]
    near, near_there = [], []
    weights = None
    for batch, rows in enumerate(payload):
        if batch:
            rows = after(rows, near[-1])
        near_there.append([own_there[batch]])
        for span in spans:
            received = mirror(rows, span)
            received = after(received, *(weights if batch else own_there))
            near_there[batch].append(to_mid(received))
            rows = join(rows, received)
        near.append(rows)
        if weights is None:
            weights = load([after(w, rows) for w in (gate_weight, up_weight, down_weight)])
    far = [mirror(rows, 2) for rows in near]
    far_there = [to_mid(rows) for rows in far]

    halves, sent, back = [], [], []
    for batch in range(batches):
        ahead = batch + 1 < batches
        for at, xs in enumerate(([near[batch], *near_there[batch]], [far[batch], far_there[batch]])):
            xs = [*xs, *[to_core(x) for x in xs]]
            first = [near[batch + 1]] if ahead and at == 0 else []
            xs[0] = after(xs[0], *first, *sent[-1:])
            mine, other = ffn(xs, table, weights)
            wait = []
            if ahead:
                wait = [far_there[batch + 1]]
                if at == 0:
                    wait = [far[batch + 1], far_there[batch], *near_there[batch + 1]]
            other = to_core(after(other, *wait, *back[-2:-1]))
            sent.append(total([(mine, 1, 0), (other, 1, 0)], [(0, half)])[0])
            back.append(to_mid(sent[-1]))
            halves.append([(mine, 0, 0), (other, 0, 0), (back[-1], None, 0)])

    terms = []
    for batch in range(batches):
        near_terms, far_terms = halves[2 * batch], halves[2 * batch + 1]
        parts = total(near_terms, [(j, j + 1) for j in range(1, half)])
        returned = [
            along_line(part, lambda p, j=j: owner_of(p, j, len(spans)))
            for j, part in enumerate(parts, 1)
        ]
        if batch + 1 == batches and terms:
            last = [a for a, _, _ in terms[-1][3:]] + returned
            far_terms = [*far_terms[:-1], (after(far_terms[-1][0], *last), None, 0)]
        parts = total(far_terms, [(j, j + 1) for j in range(half)])
        returned += [
            along_line(part, lambda p, j=j: owner_of(mirrored(p, 2), j, len(spans)))
            for j, part in enumerate(parts)
        ]
        terms.append(near_terms + [(part, None, 0) for part in returned])
    return finish(hidden_in, terms)


def solution(mesh):
    return jax.shard_map(
        local,
        mesh=mesh,
        in_specs=(
            P(None, ("grp", "ep"), None),
            P(None, ("grp", "ep"), None),
            P(None, ("grp", "ep"), None),
            P(),
            P("ep", None, None),
            P("ep", None, None),
            P("ep", None, None),
            P("ep", None, None),
        ),
        out_specs=P(None, ("grp", "ep"), None),
        check_vma=False,
    )
```

```python
import functools

import jax
import jax.numpy as jnp
from jax import lax
from jax.experimental import pallas as pl
from jax.experimental.pallas import tpu as pltpu
from jax.sharding import PartitionSpec as P

LANES = 128
SHARES = 4
VMEM = pl.BlockSpec(memory_space=pltpu.VMEM)
HBM = pl.BlockSpec(memory_space=pltpu.HBM)
SMEM = pl.BlockSpec(memory_space=pltpu.SMEM)
PINNED = {pltpu.VMEM, pltpu.HBM}


def call(kernel, operands, specs, shapes, scratch=(), name=None, vmem=8, pin=True):
    if pin:
        shapes = [pltpu.VMEM(s.shape, s.dtype) for s in shapes]
        operands = [
            pltpu.with_memory_space_constraint(a, spec.memory_space)
            if spec.memory_space in PINNED
            else a
            for a, spec in zip(operands, specs)
        ]
    return pl.pallas_call(
        kernel,
        out_shape=shapes,
        in_specs=specs,
        out_specs=[VMEM] * len(shapes),
        scratch_shapes=list(scratch),
        cost_estimate=pl.CostEstimate(flops=0, bytes_accessed=0, transcendentals=0),
        compiler_params=pltpu.CompilerParams(vmem_limit_bytes=vmem << 20),
        name=name,
    )(*operands)


def after(value, *others):
    return lax.optimization_barrier((value, *others))[0]


def prepare_kernel(hidden_hbm, ids_hbm, share_hbm, gain_hbm, *refs):
    out_refs, (hidden_ref, ids_ref, share_ref, gain_ref, sems) = refs[:-5], refs[-5:]
    sources = (hidden_hbm, ids_hbm, share_hbm, gain_hbm)
    targets = (hidden_ref, ids_ref, share_ref, gain_ref)
    copies = [pltpu.make_async_copy(s, t, sems.at[i]) for i, (s, t) in enumerate(zip(sources, targets))]
    for copy in copies:
        copy.start()
    for copy in copies:
        copy.wait()
    rows, width = hidden_ref.shape[1:]
    fanout = ids_ref.shape[1]
    extra = out_refs[0].shape[2] - width
    for batch, out_ref in enumerate(out_refs):
        values = hidden_ref[batch].astype(jnp.float32)
        power = jnp.mean(values * values, axis=-1, keepdims=True)
        normed = values * lax.rsqrt(power + 1e-06) * gain_ref[...]
        out_ref[0, :, :width] = normed.astype(jnp.bfloat16)
        expert = lax.broadcasted_iota(jnp.int32, (extra, rows), 0)
        dense = jnp.zeros((extra, rows), jnp.float32)
        for k in range(fanout):
            share = share_ref[batch, k : k + 1, :].astype(jnp.float32) * (1.0 / 64.0)
            dense = dense + jnp.where(expert == ids_ref[batch, k : k + 1, :], share, 0.0)
        out_ref[0, :, width:] = dense.T.astype(jnp.bfloat16)


def prepare(hidden_in, expert_ids, route_share, norm_gain, extra):
    batches, rows, width = hidden_in.shape
    operands = [
        hidden_in,
        expert_ids.transpose(0, 2, 1),
        route_share.transpose(0, 2, 1),
        norm_gain.reshape(1, width),
    ]
    return call(
        prepare_kernel,
        operands,
        [HBM] * 4,
        [jax.ShapeDtypeStruct((1, rows, width + extra), jnp.bfloat16)] * batches,
        [pltpu.VMEM(a.shape, a.dtype) for a in operands] + [pltpu.SemaphoreType.DMA((4,))],
        name="prepare",
    )


def join_kernel(*refs):
    at = 0
    for ref in refs[:-1]:
        refs[-1][at : at + ref.shape[0]] = ref[...]
        at += ref.shape[0]


def join(a, b):
    shape = jax.ShapeDtypeStruct((a.shape[0] + b.shape[0], *a.shape[1:]), a.dtype)
    return call(join_kernel, [a, b], [VMEM] * 2, [shape], name="join")[0]


def load_kernel(*refs):
    count = len(refs) // 2
    copies = [pltpu.make_async_copy(refs[i], refs[count + i], refs[-1].at[i]) for i in range(count)]
    for copy in copies:
        copy.start()
    for copy in copies:
        copy.wait()


def load(weights):
    return call(
        load_kernel,
        weights,
        [HBM] * len(weights),
        [jax.ShapeDtypeStruct(w.shape, w.dtype) for w in weights],
        [pltpu.SemaphoreType.DMA((len(weights),))],
        name="load",
    )


def ffn_kernel(table_ref, gate_ref, up_ref, down_ref, *refs):
    x_refs, outs, (x_all, hidden) = refs[: -3 - SHARES], refs[-3 - SHARES : -2], refs[-2:]
    mine_ref, other_refs = outs[0], outs[1:]
    width, ff = gate_ref.shape[1:]
    group = ff // table_ref.shape[2]
    step = 2 * group if ff % (2 * group) == 0 else group
    _, pieces, part, _ = mine_ref.shape
    at = 0
    for x_ref in x_refs:
        rows = x_ref.shape[0] * part
        x_all[at : at + rows, :] = x_ref[...].reshape(rows, x_ref.shape[2])
        at += rows

    def scale(which, b):
        return jnp.exp2(jnp.full((1, group), table_ref[which, 0, b], jnp.int32).astype(jnp.float32))

    for f in range(0, ff, step):
        x = x_all[:, :width]
        gate = jnp.dot(x, gate_ref[0, :, f : f + step], preferred_element_type=jnp.float32)
        up = jnp.dot(x, up_ref[0, :, f : f + step], preferred_element_type=jnp.float32)
        for at in range(0, step, group):
            b = (f + at) // group
            g = gate[:, at : at + group] * scale(0, b)
            u = up[:, at : at + group] * scale(1, b)
            h = g / (1.0 + jnp.exp(-g)) * u * scale(2, b)
            hidden[:, f + at : f + at + group] = h.astype(jnp.bfloat16)
    shares = x_all[:, width:].astype(jnp.float32)
    here = lax.broadcasted_iota(jnp.int32, shares.shape, 1) == lax.axis_index("ep")
    weight = jnp.sum(jnp.where(here, shares, 0.0), axis=1, keepdims=True)
    cols = 512 if width % 512 == 0 else LANES
    for n in range(0, width, cols):
        out = jnp.dot(hidden[...], down_ref[0, :, n : n + cols], preferred_element_type=jnp.float32)
        out = (out * weight).astype(jnp.bfloat16).reshape(4, pieces, part, cols)
        mine_ref[:, :, :, n : n + cols] = out[:2]
        other = out[2:].reshape(2 * pieces, part, cols)
        for i, other_ref in enumerate(other_refs):
            at = i * other_ref.shape[0]
            other_ref[:, :, n : n + cols] = other[at : at + other_ref.shape[0]]


def ffn(xs, table, weights):
    pieces = sum(x.shape[0] for x in xs) // 4
    _, part, full = xs[0].shape
    width, ff = weights[0].shape[1:]
    rows = 4 * pieces * part
    return call(
        ffn_kernel,
        [table, *weights, *xs],
        [SMEM] + [VMEM] * (3 + len(xs)),
        [jax.ShapeDtypeStruct((2, pieces, part, width), jnp.bfloat16)]
        + [jax.ShapeDtypeStruct((2 * pieces // SHARES, part, width), jnp.bfloat16)] * SHARES,
        [pltpu.VMEM((rows, full), jnp.bfloat16), pltpu.VMEM((rows, ff), jnp.bfloat16)],
        name="ffn",
        vmem=16,
    )


def piece_of(slot, refs, piece):
    if slot is not None:
        return refs[0][slot, piece]
    for ref in refs:
        if piece < ref.shape[0]:
            return ref[piece]
        piece -= ref.shape[0]


def sum_of(layout, refs, piece):
    result, at = None, 0
    for slot, skip, count in layout:
        term = piece_of(slot, refs[at : at + count], piece - skip).astype(jnp.float32)
        result = term if result is None else result + term
        at += count
    return result


def total_kernel(layout, cuts, *refs):
    ins, outs = refs[: -len(cuts)], refs[-len(cuts) :]
    for (low, high), out_ref in zip(cuts, outs):
        for piece in range(low, high):
            out_ref[piece - low] = sum_of(layout, ins, piece).astype(out_ref.dtype)


def total(terms, cuts):
    first = cuts[0][0]
    kept = []
    for slot, arrays in terms:
        skip = 0
        while slot is None and first >= skip + arrays[0].shape[0]:
            skip, arrays = skip + arrays[0].shape[0], arrays[1:]
        high = cuts[-1][1] - skip
        while slot is None and high <= sum(a.shape[0] for a in arrays[:-1]):
            arrays = arrays[:-1]
        kept.append((slot, skip, arrays))
    layout = [(slot, skip, len(arrays)) for slot, skip, arrays in kept]
    arrays = [a for _, _, arrays in kept for a in arrays]
    part, width = arrays[0].shape[-2:]
    return call(
        functools.partial(total_kernel, layout, cuts),
        arrays,
        [VMEM] * len(arrays),
        [jax.ShapeDtypeStruct((high - low, part, width), arrays[0].dtype) for low, high in cuts],
        name="total",
    )


def finish_kernel(layout, hidden_ref, *refs):
    out_ref = refs[-1]
    count = (len(refs) - 1) // hidden_ref.shape[0]
    for batch in range(hidden_ref.shape[0]):
        mixed = sum_of(layout, refs[batch * count : (batch + 1) * count], 0)
        out_ref[batch] = (hidden_ref[batch].astype(jnp.float32) + mixed).astype(out_ref.dtype)


def finish(hidden_in, terms):
    layout = [(slot, 0, 1) for slot, _ in terms[0]]
    arrays = [arrays[0] for batch in terms for _, arrays in batch]
    return call(
        functools.partial(finish_kernel, layout),
        [hidden_in, *arrays],
        [VMEM] * (1 + len(arrays)),
        [jax.ShapeDtypeStruct(hidden_in.shape, hidden_in.dtype)],
        name="finish",
        pin=False,
    )[0]


def local(
    hidden_in,
    expert_ids,
    route_share,
    norm_gain,
    gate_weight,
    up_weight,
    down_weight,
    exponent_table,
):
    owners = lax.axis_size("ep")
    batches = hidden_in.shape[0]
    table = exponent_table.transpose(1, 0, 2)

    line = owners // 4
    half = line // 2

    def along_line(rows, place_of):
        return lax.ppermute(rows, "ep", [(i, place_of(i // 4) * 4 + i % 4) for i in range(owners)])

    def mirrored(p, span):
        return p // span * span + span - 1 - p % span

    def mirror(rows, span):
        return along_line(rows, lambda p: mirrored(p, span))

    def to_mid(rows):
        return lax.ppermute(rows, "ep", [(i, i ^ 2) for i in range(owners)])

    def to_core(rows):
        return lax.ppermute(rows, "ep", [(i, i ^ 1) for i in range(owners)])

    payload = prepare(hidden_in, expert_ids, route_share, norm_gain, -(-owners // LANES) * LANES)

    own_there = [to_mid(rows) for rows in payload]
    near, far, there = [], [], []
    for batch, rows in enumerate(payload):
        if batch:
            rows = after(rows, near[-1])
        there.append([own_there[batch]])
        span = line
        while span > 2:
            received = mirror(rows, span)
            if not batch:
                received = after(received, *own_there)
            there[batch].append(to_mid(received))
            rows = join(rows, received)
            if batch:
                rows = after(rows, far[-1])
            span //= 2
        near.append(rows)
        far.append(mirror(rows if not batch else after(rows, *there[batch - 1]), 2))
    weights = load([after(w, near[-1]) for w in (gate_weight, up_weight, down_weight)])
    far[-1] = after(far[-1], *weights)
    ahead = there[-1][-1]
    for batch in range(batches):
        rows = far[batch]
        if batch + 1 < batches:
            rows = after(rows, near[batch + 1])
        there[batch].append(to_mid(rows))

    terms, sent, back = [], [], []
    for batch in range(batches):
        xs = [near[batch], far[batch], *there[batch]]
        xs += [to_core(rows) for rows in xs]
        xs[0] = after(xs[0], far[-1], ahead, *sent[-1:])
        mine, *others = ffn(xs, table, weights)
        wait = there[batch + 1] if batch + 1 < batches else []
        others = [to_core(after(other, *wait)) for other in others]
        other_here, other_there = others[: SHARES // 2], others[SHARES // 2 :]
        own = [(1, [mine]), (None, [after(other_there[0], *other_here), *other_there[1:]])]
        if batch + 1 < batches:
            sent += total(own, [(0, line)])
            back.append([to_mid(sent[-1])])
        else:
            sent += total(own, [(half, line)])
            back.append([to_mid(total(own, [(0, half)])[0]), to_mid(sent[-1])])
        terms.append([(0, [mine]), (None, other_here), (None, back[-1])])

    for batch in range(batches):
        if batch + 1 < batches:
            terms[batch][-1] = (None, [after(back[batch][0], sent[-1])])
        far_sum = total(terms[batch], [(half, line)])[0]
        terms[batch].append((None, [mirror(far_sum, 2)]))
        span, pieces = 4, half
        while pieces > 1:
            part = total(terms[batch], [(pieces // 2, pieces)])[0]
            terms[batch].append((None, [mirror(part, span)]))
            span, pieces = span * 2, pieces // 2
    return finish(hidden_in, terms)


def solution(mesh):
    return jax.shard_map(
        local,
        mesh=mesh,
        in_specs=(
            P(None, ("grp", "ep"), None),
            P(None, ("grp", "ep"), None),
            P(None, ("grp", "ep"), None),
            P(),
            P("ep", None, None),
            P("ep", None, None),
            P("ep", None, None),
            P("ep", None, None),
        ),
        out_specs=P(None, ("grp", "ep"), None),
        check_vma=False,
    )
```

```python
import functools

import jax
import jax.numpy as jnp
from jax import lax
from jax.experimental import pallas as pl
from jax.experimental.pallas import tpu as pltpu
from jax.sharding import PartitionSpec as P

LANES = 128
SHARES = 4
VMEM = pl.BlockSpec(memory_space=pltpu.VMEM)
HBM = pl.BlockSpec(memory_space=pltpu.HBM)
SMEM = pl.BlockSpec(memory_space=pltpu.SMEM)
PINNED = {pltpu.VMEM, pltpu.HBM}


def call(kernel, operands, specs, shapes, scratch=(), name=None, vmem=8, pin=True):
    if pin:
        shapes = [pltpu.VMEM(s.shape, s.dtype) for s in shapes]
        operands = [
            pltpu.with_memory_space_constraint(a, spec.memory_space)
            if spec.memory_space in PINNED
            else a
            for a, spec in zip(operands, specs)
        ]
    return pl.pallas_call(
        kernel,
        out_shape=shapes,
        in_specs=specs,
        out_specs=[VMEM] * len(shapes),
        scratch_shapes=list(scratch),
        cost_estimate=pl.CostEstimate(flops=0, bytes_accessed=0, transcendentals=0),
        compiler_params=pltpu.CompilerParams(vmem_limit_bytes=vmem << 20),
        name=name,
    )(*operands)


def after(value, *others):
    return lax.optimization_barrier((value, *others))[0]


def prepare_kernel(hidden_hbm, ids_hbm, share_hbm, gain_hbm, *refs):
    out_refs, (hidden_ref, ids_ref, share_ref, gain_ref, sems) = refs[:-5], refs[-5:]
    sources = (hidden_hbm, ids_hbm, share_hbm, gain_hbm)
    targets = (hidden_ref, ids_ref, share_ref, gain_ref)
    copies = [pltpu.make_async_copy(s, t, sems.at[i]) for i, (s, t) in enumerate(zip(sources, targets))]
    for copy in copies:
        copy.start()
    for copy in copies:
        copy.wait()
    rows, width = hidden_ref.shape[1:]
    fanout = ids_ref.shape[1]
    extra = out_refs[0].shape[2] - width
    for batch, out_ref in enumerate(out_refs):
        values = hidden_ref[batch].astype(jnp.float32)
        power = jnp.mean(values * values, axis=-1, keepdims=True)
        normed = values * lax.rsqrt(power + 1e-06) * gain_ref[...]
        out_ref[0, :, :width] = normed.astype(jnp.bfloat16)
        expert = lax.broadcasted_iota(jnp.int32, (extra, rows), 0)
        dense = jnp.zeros((extra, rows), jnp.float32)
        for k in range(fanout):
            share = share_ref[batch, k : k + 1, :].astype(jnp.float32) * (1.0 / 64.0)
            dense = dense + jnp.where(expert == ids_ref[batch, k : k + 1, :], share, 0.0)
        out_ref[0, :, width:] = dense.T.astype(jnp.bfloat16)


def prepare(hidden_in, expert_ids, route_share, norm_gain, extra):
    batches, rows, width = hidden_in.shape
    operands = [
        hidden_in,
        expert_ids.transpose(0, 2, 1),
        route_share.transpose(0, 2, 1),
        norm_gain.reshape(1, width),
    ]
    return call(
        prepare_kernel,
        operands,
        [HBM] * 4,
        [jax.ShapeDtypeStruct((1, rows, width + extra), jnp.bfloat16)] * batches,
        [pltpu.VMEM(a.shape, a.dtype) for a in operands] + [pltpu.SemaphoreType.DMA((4,))],
        name="prepare",
    )


def join_kernel(*refs):
    at = 0
    for ref in refs[:-1]:
        refs[-1][at : at + ref.shape[0]] = ref[...]
        at += ref.shape[0]


def join(a, b):
    shape = jax.ShapeDtypeStruct((a.shape[0] + b.shape[0], *a.shape[1:]), a.dtype)
    return call(join_kernel, [a, b], [VMEM] * 2, [shape], name="join")[0]


def load_kernel(*refs):
    count = len(refs) // 2
    copies = [pltpu.make_async_copy(refs[i], refs[count + i], refs[-1].at[i]) for i in range(count)]
    for copy in copies:
        copy.start()
    for copy in copies:
        copy.wait()


def load(weights):
    return call(
        load_kernel,
        weights,
        [HBM] * len(weights),
        [jax.ShapeDtypeStruct(w.shape, w.dtype) for w in weights],
        [pltpu.SemaphoreType.DMA((len(weights),))],
        name="load",
    )


def ffn_kernel(table_ref, gate_ref, up_ref, down_ref, *refs):
    x_refs, outs, (x_all, hidden) = refs[: -3 - SHARES], refs[-3 - SHARES : -2], refs[-2:]
    mine_ref, other_refs = outs[0], outs[1:]
    width, ff = gate_ref.shape[1:]
    group = ff // table_ref.shape[2]
    step = 2 * group if ff % (2 * group) == 0 else group
    _, pieces, part, _ = mine_ref.shape
    at = 0
    for x_ref in x_refs:
        rows = x_ref.shape[0] * part
        x_all[at : at + rows, :] = x_ref[...].reshape(rows, x_ref.shape[2])
        at += rows

    def scale(which, b):
        return jnp.exp2(jnp.full((1, group), table_ref[which, 0, b], jnp.int32).astype(jnp.float32))

    for f in range(0, ff, step):
        x = x_all[:, :width]
        gate = jnp.dot(x, gate_ref[0, :, f : f + step], preferred_element_type=jnp.float32)
        up = jnp.dot(x, up_ref[0, :, f : f + step], preferred_element_type=jnp.float32)
        for at in range(0, step, group):
            b = (f + at) // group
            g = gate[:, at : at + group] * scale(0, b)
            u = up[:, at : at + group] * scale(1, b)
            h = g / (1.0 + jnp.exp(-g)) * u * scale(2, b)
            hidden[:, f + at : f + at + group] = h.astype(jnp.bfloat16)
    shares = x_all[:, width:].astype(jnp.float32)
    here = lax.broadcasted_iota(jnp.int32, shares.shape, 1) == lax.axis_index("ep")
    weight = jnp.sum(jnp.where(here, shares, 0.0), axis=1, keepdims=True)
    cols = 512 if width % 512 == 0 else LANES
    for n in range(0, width, cols):
        out = jnp.dot(hidden[...], down_ref[0, :, n : n + cols], preferred_element_type=jnp.float32)
        out = (out * weight).astype(jnp.bfloat16).reshape(4, pieces, part, cols)
        mine_ref[:, :, :, n : n + cols] = out[:2]
        other = out[2:].reshape(2 * pieces, part, cols)
        for i, other_ref in enumerate(other_refs):
            at = i * other_ref.shape[0]
            other_ref[:, :, n : n + cols] = other[at : at + other_ref.shape[0]]


def ffn(xs, table, weights):
    pieces = sum(x.shape[0] for x in xs) // 4
    _, part, full = xs[0].shape
    width, ff = weights[0].shape[1:]
    rows = 4 * pieces * part
    return call(
        ffn_kernel,
        [table, *weights, *xs],
        [SMEM] + [VMEM] * (3 + len(xs)),
        [jax.ShapeDtypeStruct((2, pieces, part, width), jnp.bfloat16)]
        + [jax.ShapeDtypeStruct((2 * pieces // SHARES, part, width), jnp.bfloat16)] * SHARES,
        [pltpu.VMEM((rows, full), jnp.bfloat16), pltpu.VMEM((rows, ff), jnp.bfloat16)],
        name="ffn",
        vmem=16,
    )


def piece_of(slot, refs, piece):
    if slot is not None:
        return refs[0][slot, piece]
    for ref in refs:
        if piece < ref.shape[0]:
            return ref[piece]
        piece -= ref.shape[0]


def sum_of(layout, refs, piece):
    result, at = None, 0
    for slot, skip, count in layout:
        term = piece_of(slot, refs[at : at + count], piece - skip).astype(jnp.float32)
        result = term if result is None else result + term
        at += count
    return result


def narrow(terms, low, high):
    layout, kept = [], []
    for slot, arrays, *first in terms:
        skip = -first[0] if first else 0
        while slot is None and low >= skip + arrays[0].shape[0]:
            skip, arrays = skip + arrays[0].shape[0], arrays[1:]
        while slot is None and high <= skip + sum(a.shape[0] for a in arrays[:-1]):
            arrays = arrays[:-1]
        layout.append((slot, skip, len(arrays)))
        kept += arrays
    return layout, kept


def total_kernel(layout, cuts, *refs):
    ins, outs = refs[: -len(cuts)], refs[-len(cuts) :]
    for (low, high), out_ref in zip(cuts, outs):
        for piece in range(low, high):
            out_ref[piece - low] = sum_of(layout, ins, piece).astype(out_ref.dtype)


def total(terms, cuts):
    layout, kept = narrow(terms, cuts[0][0], cuts[-1][1])
    part, width = kept[0].shape[-2:]
    return call(
        functools.partial(total_kernel, layout, cuts),
        kept,
        [VMEM] * len(kept),
        [jax.ShapeDtypeStruct((high - low, part, width), kept[0].dtype) for low, high in cuts],
        name="total",
    )


def finish_kernel(layouts, hidden_ref, *refs):
    out_ref = refs[-1]
    count = (len(refs) - 1) // hidden_ref.shape[0]
    for batch in range(hidden_ref.shape[0]):
        mixed = sum_of(layouts[batch], refs[batch * count : (batch + 1) * count], 0)
        out_ref[batch] = (hidden_ref[batch].astype(jnp.float32) + mixed).astype(out_ref.dtype)


def finish(hidden_in, terms):
    layouts, arrays = [], []
    for batch in terms:
        layout, kept = narrow(batch, 0, 1)
        layouts.append(layout)
        arrays += kept
    return call(
        functools.partial(finish_kernel, layouts),
        [hidden_in, *arrays],
        [VMEM] * (1 + len(arrays)),
        [jax.ShapeDtypeStruct(hidden_in.shape, hidden_in.dtype)],
        name="finish",
        pin=False,
    )[0]


def local(
    hidden_in,
    expert_ids,
    route_share,
    norm_gain,
    gate_weight,
    up_weight,
    down_weight,
    exponent_table,
):
    owners = lax.axis_size("ep")
    batches = hidden_in.shape[0]
    table = exponent_table.transpose(1, 0, 2)

    line = owners // 4
    half = line // 2

    def along_line(rows, place_of):
        return lax.ppermute(rows, "ep", [(i, place_of(i // 4) * 4 + i % 4) for i in range(owners)])

    def mirrored(p, span):
        return p // span * span + span - 1 - p % span

    def mirror(rows, span):
        return along_line(rows, lambda p: mirrored(p, span))

    def to_mid(rows):
        return lax.ppermute(rows, "ep", [(i, i ^ 2) for i in range(owners)])

    def to_core(rows):
        return lax.ppermute(rows, "ep", [(i, i ^ 1) for i in range(owners)])

    spans = []
    while line >> len(spans) > 2:
        spans.append(line >> len(spans))

    def owner_of(p, piece):
        for level in range(len(spans), 0, -1):
            if piece >= 1 << (level - 1):
                p, piece = mirrored(p, spans[level - 1]), piece - (1 << (level - 1))
        return p

    payload = prepare(hidden_in, expert_ids, route_share, norm_gain, -(-owners // LANES) * LANES)

    own_there = [to_mid(rows) for rows in payload]
    near, near_there, joined, far = [], [], [], []
    weights = None
    for batch, rows in enumerate(payload):
        if batch:
            rows = after(rows, joined[-1])
        near.append([rows])
        near_there.append([own_there[batch]])
        for span in spans:
            received = mirror(rows, span)
            received = after(received, *([*weights, far[-1]] if batch else own_there))
            near[batch].append(received)
            near_there[batch].append(to_mid(received))
            rows = join(rows, received)
        joined.append(rows)
        far.append(mirror(rows, 2))
        if weights is None:
            weights = load([after(w, rows) for w in (gate_weight, up_weight, down_weight)])
    far_there = [to_mid(rows) for rows in far]

    groups = [[(0, 0)]]
    for batch in range(batches):
        groups.append([(batch, 1)] + [(batch + 1, 0)] * (batch + 1 < batches))
    order, wait = joined[1:2], far[1:2] + [x for xs in near_there[1:2] for x in xs]
    sums, back, arrived = {}, {}, []
    for group in groups:
        here = [x for batch, is_far in group for x in ([far[batch]] if is_far else near[batch])]
        there = [x for batch, is_far in group for x in ([far_there[batch]] if is_far else near_there[batch])]
        xs = [*here, *there]
        xs += [to_core(x) for x in xs]
        mine, *others = ffn([after(xs[0], *order), *xs[1:]], table, weights)
        others = [to_core(after(other, *wait)) for other in others]
        other_here, other_there = others[: SHARES // 2], others[SHARES // 2 :]
        own = [(1, [mine]), (None, [after(other_there[0], *other_here), *other_there[1:]])]
        order, arrived = [], []
        for i, unit in enumerate(group):
            cut = (i * half, (i + 1) * half)
            sent = total(own, [cut])[0]
            back[unit] = to_mid(sent)
            order.append(sent)
            arrived.append(back[unit])
            sums[unit] = ([(0, [mine]), (None, other_here)], cut[0])
        batch, is_far = group[-1]
        wait = [arrived[0], *far_there[batch + 1 : batch + 2]] if not is_far else arrived[:1]

    terms, last = [[] for _ in range(batches)], []
    for unit in [unit for group in groups for unit in group]:
        batch, is_far = unit
        own, first = sums[unit]
        own = [(slot, arrays, first) for slot, arrays in own] + [(None, [after(back[unit], *last)], 0)]
        skip = 0 if is_far else 1
        parts = total(own, [(j, j + 1) for j in range(skip, half)])
        returned = [
            along_line(part, lambda p, j=j: owner_of(mirrored(p, 2) if is_far else p, j))
            for j, part in enumerate(parts, skip)
        ]
        if not is_far:
            terms[batch] += own
        terms[batch] += [(None, [part], 0) for part in returned]
        last = returned
    return finish(hidden_in, terms)


def solution(mesh):
    return jax.shard_map(
        local,
        mesh=mesh,
        in_specs=(
            P(None, ("grp", "ep"), None),
            P(None, ("grp", "ep"), None),
            P(None, ("grp", "ep"), None),
            P(),
            P("ep", None, None),
            P("ep", None, None),
            P("ep", None, None),
            P("ep", None, None),
        ),
        out_specs=P(None, ("grp", "ep"), None),
        check_vma=False,
    )
```

```python
import functools

import jax
import jax.numpy as jnp
from jax import lax
from jax.experimental import pallas as pl
from jax.experimental.pallas import tpu as pltpu
from jax.sharding import PartitionSpec as P

LANES = 128
SHARES = 4
VMEM = pl.BlockSpec(memory_space=pltpu.VMEM)
HBM = pl.BlockSpec(memory_space=pltpu.HBM)
SMEM = pl.BlockSpec(memory_space=pltpu.SMEM)
PINNED = {pltpu.VMEM, pltpu.HBM}


def call(kernel, operands, specs, shapes, scratch=(), name=None, vmem=8, pin=True):
    if pin:
        shapes = [pltpu.VMEM(s.shape, s.dtype) for s in shapes]
        operands = [
            pltpu.with_memory_space_constraint(a, spec.memory_space)
            if spec.memory_space in PINNED
            else a
            for a, spec in zip(operands, specs)
        ]
    return pl.pallas_call(
        kernel,
        out_shape=shapes,
        in_specs=specs,
        out_specs=[VMEM] * len(shapes),
        scratch_shapes=list(scratch),
        cost_estimate=pl.CostEstimate(flops=0, bytes_accessed=0, transcendentals=0),
        compiler_params=pltpu.CompilerParams(vmem_limit_bytes=vmem << 20),
        name=name,
    )(*operands)


def after(value, *others):
    return lax.optimization_barrier((value, *others))[0]


def prepare_kernel(hidden_hbm, ids_hbm, share_hbm, gain_hbm, *refs):
    out_refs, (hidden_ref, ids_ref, share_ref, gain_ref, sems) = refs[:-5], refs[-5:]
    sources = (hidden_hbm, ids_hbm, share_hbm, gain_hbm)
    targets = (hidden_ref, ids_ref, share_ref, gain_ref)
    copies = [pltpu.make_async_copy(s, t, sems.at[i]) for i, (s, t) in enumerate(zip(sources, targets))]
    for copy in copies:
        copy.start()
    for copy in copies:
        copy.wait()
    rows, width = hidden_ref.shape[1:]
    fanout = ids_ref.shape[1]
    extra = out_refs[0].shape[2] - width
    for batch, out_ref in enumerate(out_refs):
        values = hidden_ref[batch].astype(jnp.float32)
        power = jnp.mean(values * values, axis=-1, keepdims=True)
        normed = values * lax.rsqrt(power + 1e-06) * gain_ref[...]
        out_ref[0, :, :width] = normed.astype(jnp.bfloat16)
        expert = lax.broadcasted_iota(jnp.int32, (extra, rows), 0)
        dense = jnp.zeros((extra, rows), jnp.float32)
        for k in range(fanout):
            share = share_ref[batch, k : k + 1, :].astype(jnp.float32) * (1.0 / 64.0)
            dense = dense + jnp.where(expert == ids_ref[batch, k : k + 1, :], share, 0.0)
        out_ref[0, :, width:] = dense.T.astype(jnp.bfloat16)


def prepare(hidden_in, expert_ids, route_share, norm_gain, extra):
    batches, rows, width = hidden_in.shape
    operands = [
        hidden_in,
        expert_ids.transpose(0, 2, 1),
        route_share.transpose(0, 2, 1),
        norm_gain.reshape(1, width),
    ]
    return call(
        prepare_kernel,
        operands,
        [HBM] * 4,
        [jax.ShapeDtypeStruct((1, rows, width + extra), jnp.bfloat16)] * batches,
        [pltpu.VMEM(a.shape, a.dtype) for a in operands] + [pltpu.SemaphoreType.DMA((4,))],
        name="prepare",
    )


def join_kernel(*refs):
    at = 0
    for ref in refs[:-1]:
        refs[-1][at : at + ref.shape[0]] = ref[...]
        at += ref.shape[0]


def join(pieces):
    shape = (sum(p.shape[0] for p in pieces), *pieces[0].shape[1:])
    shape = jax.ShapeDtypeStruct(shape, pieces[0].dtype)
    return call(join_kernel, pieces, [VMEM] * len(pieces), [shape], name="join")[0]


def load_kernel(*refs):
    count = len(refs) // 2
    copies = [pltpu.make_async_copy(refs[i], refs[count + i], refs[-1].at[i]) for i in range(count)]
    for copy in copies:
        copy.start()
    for copy in copies:
        copy.wait()


def load(weights):
    return call(
        load_kernel,
        weights,
        [HBM] * len(weights),
        [jax.ShapeDtypeStruct(w.shape, w.dtype) for w in weights],
        [pltpu.SemaphoreType.DMA((len(weights),))],
        name="load",
    )


def ffn_kernel(table_ref, gate_ref, up_ref, down_ref, *refs):
    x_refs, outs, (x_all, hidden) = refs[: -3 - SHARES], refs[-3 - SHARES : -2], refs[-2:]
    mine_ref, other_refs = outs[0], outs[1:]
    width, ff = gate_ref.shape[1:]
    group = ff // table_ref.shape[2]
    step = 2 * group if ff % (2 * group) == 0 else group
    _, pieces, part, _ = mine_ref.shape
    at = 0
    for x_ref in x_refs:
        rows = x_ref.shape[0] * part
        x_all[at : at + rows, :] = x_ref[...].reshape(rows, x_ref.shape[2])
        at += rows

    def scale(which, b):
        return jnp.exp2(jnp.full((1, group), table_ref[which, 0, b], jnp.int32).astype(jnp.float32))

    for f in range(0, ff, step):
        x = x_all[:, :width]
        gate = jnp.dot(x, gate_ref[0, :, f : f + step], preferred_element_type=jnp.float32)
        up = jnp.dot(x, up_ref[0, :, f : f + step], preferred_element_type=jnp.float32)
        for at in range(0, step, group):
            b = (f + at) // group
            g = gate[:, at : at + group] * scale(0, b)
            u = up[:, at : at + group] * scale(1, b)
            h = g / (1.0 + jnp.exp(-g)) * u * scale(2, b)
            hidden[:, f + at : f + at + group] = h.astype(jnp.bfloat16)
    shares = x_all[:, width:].astype(jnp.float32)
    here = lax.broadcasted_iota(jnp.int32, shares.shape, 1) == lax.axis_index("ep")
    weight = jnp.sum(jnp.where(here, shares, 0.0), axis=1, keepdims=True)
    cols = 512 if width % 512 == 0 else LANES
    for n in range(0, width, cols):
        out = jnp.dot(hidden[...], down_ref[0, :, n : n + cols], preferred_element_type=jnp.float32)
        out = (out * weight).astype(jnp.bfloat16).reshape(4, pieces, part, cols)
        mine_ref[:, :, :, n : n + cols] = out[:2]
        other = out[2:].reshape(2 * pieces, part, cols)
        for i, other_ref in enumerate(other_refs):
            at = i * other_ref.shape[0]
            other_ref[:, :, n : n + cols] = other[at : at + other_ref.shape[0]]


def ffn(xs, table, weights):
    pieces = sum(x.shape[0] for x in xs) // 4
    _, part, full = xs[0].shape
    width, ff = weights[0].shape[1:]
    rows = 4 * pieces * part
    return call(
        ffn_kernel,
        [table, *weights, *xs],
        [SMEM] + [VMEM] * (3 + len(xs)),
        [jax.ShapeDtypeStruct((2, pieces, part, width), jnp.bfloat16)]
        + [jax.ShapeDtypeStruct((2 * pieces // SHARES, part, width), jnp.bfloat16)] * SHARES,
        [pltpu.VMEM((rows, full), jnp.bfloat16), pltpu.VMEM((rows, ff), jnp.bfloat16)],
        name="ffn",
        vmem=16,
    )


def pieces_in(slot, array):
    return array.shape[0 if slot is None else 1]


def sum_of(layout, refs, piece):
    result, at = None, 0
    for slot, skip, count in layout:
        i = piece - skip
        for ref in refs[at : at + count]:
            if 0 <= i < pieces_in(slot, ref):
                term = (ref[i] if slot is None else ref[slot, i]).astype(jnp.float32)
                result = term if result is None else result + term
            i -= pieces_in(slot, ref)
        at += count
    return result


def narrow(terms, low, high):
    layout, kept = [], []
    for slot, arrays in terms:
        skip = 0
        while low >= skip + pieces_in(slot, arrays[0]):
            skip, arrays = skip + pieces_in(slot, arrays[0]), arrays[1:]
        while high <= skip + sum(pieces_in(slot, a) for a in arrays[:-1]):
            arrays = arrays[:-1]
        layout.append((slot, skip, len(arrays)))
        kept += arrays
    return layout, kept


def total_kernel(layout, cuts, *refs):
    ins, outs = refs[: -len(cuts)], refs[-len(cuts) :]
    for (low, high), out_ref in zip(cuts, outs):
        for piece in range(low, high):
            out_ref[piece - low] = sum_of(layout, ins, piece).astype(out_ref.dtype)


def total(terms, cuts):
    layout, kept = narrow(terms, cuts[0][0], cuts[-1][1])
    part, width = kept[0].shape[-2:]
    return call(
        functools.partial(total_kernel, layout, cuts),
        kept,
        [VMEM] * len(kept),
        [jax.ShapeDtypeStruct((high - low, part, width), kept[0].dtype) for low, high in cuts],
        name="total",
    )


def finish_kernel(layouts, hidden_ref, *refs):
    out_ref, at = refs[-1], 0
    for batch, layout in enumerate(layouts):
        mixed = sum_of(layout, refs[at:-1], 0)
        out_ref[batch] = (hidden_ref[batch].astype(jnp.float32) + mixed).astype(out_ref.dtype)
        at += sum(count for _, _, count in layout)


def finish(hidden_in, terms):
    layouts, arrays = [], []
    for batch in terms:
        layout, kept = narrow(batch, 0, 1)
        layouts.append(layout)
        arrays += kept
    return call(
        functools.partial(finish_kernel, layouts),
        [hidden_in, *arrays],
        [VMEM] * (1 + len(arrays)),
        [jax.ShapeDtypeStruct(hidden_in.shape, hidden_in.dtype)],
        name="finish",
        pin=False,
    )[0]


def local(
    hidden_in,
    expert_ids,
    route_share,
    norm_gain,
    gate_weight,
    up_weight,
    down_weight,
    exponent_table,
):
    owners = lax.axis_size("ep")
    batches = hidden_in.shape[0]
    table = exponent_table.transpose(1, 0, 2)

    line = owners // 4
    half = line // 2

    def along_line(rows, place_of):
        return lax.ppermute(rows, "ep", [(i, place_of(i // 4) * 4 + i % 4) for i in range(owners)])

    def mirrored(p, span):
        return p // span * span + span - 1 - p % span

    def mirror(rows, span):
        return along_line(rows, lambda p: mirrored(p, span))

    def to_mid(rows):
        return lax.ppermute(rows, "ep", [(i, i ^ 2) for i in range(owners)])

    def to_core(rows):
        return lax.ppermute(rows, "ep", [(i, i ^ 1) for i in range(owners)])

    spans = []
    while line >> len(spans) > 2:
        spans.append(line >> len(spans))

    def owner_of(p, piece):
        if piece >= half:
            p, piece = mirrored(p, 2), piece - half
        for level in range(len(spans), 0, -1):
            if piece >= 1 << (level - 1):
                p, piece = mirrored(p, spans[level - 1]), piece - (1 << (level - 1))
        return p

    payload = prepare(hidden_in, expert_ids, route_share, norm_gain, -(-owners // LANES) * LANES)

    weights = load([gate_weight, up_weight, down_weight])
    there = [[to_mid(rows)] for rows in payload]
    near, far, joined = [], [], []
    for batch, rows in enumerate(payload):
        if batch:
            rows = after(rows, joined[-1])
        near.append([rows])
        for span in spans:
            received = mirror(rows, span)
            received = after(received, *([far[-1]] if batch else [*weights, *[x for xs in there for x in xs]]))
            near[batch].append(received)
            rows = join([rows, received])
            if not batch:
                there[batch].append(to_mid(received))
        joined.append(rows)
        far.append(mirror(rows if not batch else after(rows, *there[0]), 2))
    for batch in range(batches):
        there[batch].append(to_mid(join([*near[batch][1:], far[batch]]) if batch else far[batch]))

    def swap(arrays):
        return [to_core(x) for x in arrays]

    def sums(calls, slot):
        other = []
        for _, shares in calls:
            count = len(shares) // 2
            other += shares[slot * count : (slot + 1) * count]
        return [(slot, [mine for mine, _ in calls]), (None, other)]

    early = [[*near[batch], far[batch], *there[batch][:-1]] for batch in range(batches)]
    early_core = [swap(xs) if batch else None for batch, xs in enumerate(early)]
    terms, sent, back = [], [], []
    for batch in range(batches):
        order = [x for xs in early_core[batch + 1 : batch + 2] for x in xs]
        calls = []
        if batch == 0:
            xs = [*near[0], *there[0][:-1]]
            mine, *other = ffn([after(xs[0], *joined[1:2]), *xs[1:], *swap(xs)], table, weights)
            calls.append((mine, swap(other)))
            xs = [far[0], after(there[0][-1], mine)]
            xs += swap(xs)
            order += calls[0][1]
        else:
            late = after(there[batch][-1], sent[-1])
            xs = [*early[batch], late, *early_core[batch], to_core(late)]
            order += calls_before[-1][1][: SHARES // 2]
        mine, *other = ffn([after(xs[0], *order), *xs[1:]], table, weights)
        calls.append((mine, swap(other)))
        calls_before = calls
        out = sums(calls, 1)
        if batch + 1 < batches:
            sent += total(out, [(0, line)])
            back.append([to_mid(sent[-1])])
        else:
            sent += total(out, [(half, line)])
            back.append([to_mid(total(out, [(0, half)])[0]), to_mid(sent[-1])])
        terms.append([*sums(calls, 0), (None, back[-1])])

    for batch in range(batches):
        mixed = terms[batch]
        if batch + 1 < batches:
            mixed[-1] = (None, [after(back[batch][0], sent[-1])])
            mixed.append((None, [mirror(total(mixed, [(half, line)])[0], 2)]))
            span, pieces = 4, half
            while pieces > 1:
                mixed.append((None, [mirror(total(mixed, [(pieces // 2, pieces)])[0], span)]))
                span, pieces = span * 2, pieces // 2
        else:
            far_parts = total(mixed, [(j, j + 1) for j in range(half, line)])
            mixed[-1] = (None, [after(mixed[-1][1][0], *far_parts), *mixed[-1][1][1:]])
            parts = total(mixed, [(j, j + 1) for j in range(1, half)]) + far_parts
            mixed += [
                (None, [along_line(part, lambda p, j=j: owner_of(p, j))]) for j, part in enumerate(parts, 1)
            ]
    return finish(hidden_in, terms)


def solution(mesh):
    return jax.shard_map(
        local,
        mesh=mesh,
        in_specs=(
            P(None, ("grp", "ep"), None),
            P(None, ("grp", "ep"), None),
            P(None, ("grp", "ep"), None),
            P(),
            P("ep", None, None),
            P("ep", None, None),
            P("ep", None, None),
            P("ep", None, None),
        ),
        out_specs=P(None, ("grp", "ep"), None),
        check_vma=False,
    )
```

```python
import functools

import jax
import jax.numpy as jnp
from jax import lax
from jax.experimental import pallas as pl
from jax.experimental.pallas import tpu as pltpu
from jax.sharding import PartitionSpec as P

LANES = 128
SHARES = 4
VMEM = pl.BlockSpec(memory_space=pltpu.VMEM)
HBM = pl.BlockSpec(memory_space=pltpu.HBM)
SMEM = pl.BlockSpec(memory_space=pltpu.SMEM)
PINNED = {pltpu.VMEM, pltpu.HBM}


def call(kernel, operands, specs, shapes, scratch=(), name=None, vmem=8, pin=True):
    if pin:
        shapes = [pltpu.VMEM(s.shape, s.dtype) for s in shapes]
        operands = [
            pltpu.with_memory_space_constraint(a, spec.memory_space)
            if spec.memory_space in PINNED
            else a
            for a, spec in zip(operands, specs)
        ]
    return pl.pallas_call(
        kernel,
        out_shape=shapes,
        in_specs=specs,
        out_specs=[VMEM] * len(shapes),
        scratch_shapes=list(scratch),
        cost_estimate=pl.CostEstimate(flops=0, bytes_accessed=0, transcendentals=0),
        compiler_params=pltpu.CompilerParams(vmem_limit_bytes=vmem << 20),
        name=name,
    )(*operands)


def after(value, *others):
    return lax.optimization_barrier((value, *others))[0]


def prepare_kernel(hidden_hbm, ids_hbm, share_hbm, gain_hbm, *refs):
    out_refs, (hidden_ref, ids_ref, share_ref, gain_ref, sems) = refs[:-5], refs[-5:]
    sources = (hidden_hbm, ids_hbm, share_hbm, gain_hbm)
    targets = (hidden_ref, ids_ref, share_ref, gain_ref)
    copies = [pltpu.make_async_copy(s, t, sems.at[i]) for i, (s, t) in enumerate(zip(sources, targets))]
    for copy in copies:
        copy.start()
    for copy in copies:
        copy.wait()
    rows, width = hidden_ref.shape[1:]
    fanout = ids_ref.shape[1]
    extra = out_refs[0].shape[2] - width
    for batch, out_ref in enumerate(out_refs):
        values = hidden_ref[batch].astype(jnp.float32)
        power = jnp.mean(values * values, axis=-1, keepdims=True)
        normed = values * lax.rsqrt(power + 1e-06) * gain_ref[...]
        out_ref[0, :, :width] = normed.astype(jnp.bfloat16)
        expert = lax.broadcasted_iota(jnp.int32, (extra, rows), 0)
        dense = jnp.zeros((extra, rows), jnp.float32)
        for k in range(fanout):
            share = share_ref[batch, k : k + 1, :].astype(jnp.float32) * (1.0 / 64.0)
            dense = dense + jnp.where(expert == ids_ref[batch, k : k + 1, :], share, 0.0)
        out_ref[0, :, width:] = dense.T.astype(jnp.bfloat16)


def prepare(hidden_in, expert_ids, route_share, norm_gain, extra):
    batches, rows, width = hidden_in.shape
    operands = [
        hidden_in,
        expert_ids.transpose(0, 2, 1),
        route_share.transpose(0, 2, 1),
        norm_gain.reshape(1, width),
    ]
    return call(
        prepare_kernel,
        operands,
        [HBM] * 4,
        [jax.ShapeDtypeStruct((1, rows, width + extra), jnp.bfloat16)] * batches,
        [pltpu.VMEM(a.shape, a.dtype) for a in operands] + [pltpu.SemaphoreType.DMA((4,))],
        name="prepare",
    )


def join_kernel(*refs):
    at = 0
    for ref in refs[:-1]:
        refs[-1][at : at + ref.shape[0]] = ref[...]
        at += ref.shape[0]


def join(pieces):
    shape = (sum(p.shape[0] for p in pieces), *pieces[0].shape[1:])
    shape = jax.ShapeDtypeStruct(shape, pieces[0].dtype)
    return call(join_kernel, pieces, [VMEM] * len(pieces), [shape], name="join")[0]


def load_kernel(*refs):
    count = len(refs) // 2
    copies = [pltpu.make_async_copy(refs[i], refs[count + i], refs[-1].at[i]) for i in range(count)]
    for copy in copies:
        copy.start()
    for copy in copies:
        copy.wait()


def load(weights):
    return call(
        load_kernel,
        weights,
        [HBM] * len(weights),
        [jax.ShapeDtypeStruct(w.shape, w.dtype) for w in weights],
        [pltpu.SemaphoreType.DMA((len(weights),))],
        name="load",
    )


def ffn_kernel(table_ref, gate_ref, up_ref, down_ref, *refs):
    x_refs, outs, (x_all, hidden) = refs[: -3 - SHARES], refs[-3 - SHARES : -2], refs[-2:]
    mine_ref, other_refs = outs[0], outs[1:]
    width, ff = gate_ref.shape[1:]
    group = ff // table_ref.shape[2]
    step = 2 * group if ff % (2 * group) == 0 else group
    _, pieces, part, _ = mine_ref.shape
    at = 0
    for x_ref in x_refs:
        rows = x_ref.shape[0] * part
        x_all[at : at + rows, :] = x_ref[...].reshape(rows, x_ref.shape[2])
        at += rows

    def scale(which, b):
        return jnp.exp2(jnp.full((1, group), table_ref[which, 0, b], jnp.int32).astype(jnp.float32))

    for f in range(0, ff, step):
        x = x_all[:, :width]
        gate = jnp.dot(x, gate_ref[0, :, f : f + step], preferred_element_type=jnp.float32)
        up = jnp.dot(x, up_ref[0, :, f : f + step], preferred_element_type=jnp.float32)
        for at in range(0, step, group):
            b = (f + at) // group
            g = gate[:, at : at + group] * scale(0, b)
            u = up[:, at : at + group] * scale(1, b)
            h = g / (1.0 + jnp.exp(-g)) * u * scale(2, b)
            hidden[:, f + at : f + at + group] = h.astype(jnp.bfloat16)
    shares = x_all[:, width:].astype(jnp.float32)
    here = lax.broadcasted_iota(jnp.int32, shares.shape, 1) == lax.axis_index("ep")
    weight = jnp.sum(jnp.where(here, shares, 0.0), axis=1, keepdims=True)
    cols = 512 if width % 512 == 0 else LANES
    for n in range(0, width, cols):
        out = jnp.dot(hidden[...], down_ref[0, :, n : n + cols], preferred_element_type=jnp.float32)
        out = (out * weight).astype(jnp.bfloat16).reshape(4, pieces, part, cols)
        mine_ref[:, :, :, n : n + cols] = out[:2]
        other = out[2:].reshape(2 * pieces, part, cols)
        for i, other_ref in enumerate(other_refs):
            at = i * other_ref.shape[0]
            other_ref[:, :, n : n + cols] = other[at : at + other_ref.shape[0]]


def ffn(xs, table, weights):
    pieces = sum(x.shape[0] for x in xs) // 4
    _, part, full = xs[0].shape
    width, ff = weights[0].shape[1:]
    rows = 4 * pieces * part
    return call(
        ffn_kernel,
        [table, *weights, *xs],
        [SMEM] + [VMEM] * (3 + len(xs)),
        [jax.ShapeDtypeStruct((2, pieces, part, width), jnp.bfloat16)]
        + [jax.ShapeDtypeStruct((2 * pieces // SHARES, part, width), jnp.bfloat16)] * SHARES,
        [pltpu.VMEM((rows, full), jnp.bfloat16), pltpu.VMEM((rows, ff), jnp.bfloat16)],
        name="ffn",
        vmem=16,
    )


def pieces_in(slot, array):
    return array.shape[0 if slot is None else 1]


def sum_of(layout, refs, piece):
    result, at = None, 0
    for slot, skip, count in layout:
        i = piece - skip
        for ref in refs[at : at + count]:
            if 0 <= i < pieces_in(slot, ref):
                term = (ref[i] if slot is None else ref[slot, i]).astype(jnp.float32)
                result = term if result is None else result + term
            i -= pieces_in(slot, ref)
        at += count
    return result


def narrow(terms, low, high):
    layout, kept = [], []
    for slot, arrays in terms:
        skip = 0
        while low >= skip + pieces_in(slot, arrays[0]):
            skip, arrays = skip + pieces_in(slot, arrays[0]), arrays[1:]
        while high <= skip + sum(pieces_in(slot, a) for a in arrays[:-1]):
            arrays = arrays[:-1]
        layout.append((slot, skip, len(arrays)))
        kept += arrays
    return layout, kept


def total_kernel(layout, cuts, *refs):
    ins, outs = refs[: -len(cuts)], refs[-len(cuts) :]
    for (low, high), out_ref in zip(cuts, outs):
        for piece in range(low, high):
            out_ref[piece - low] = sum_of(layout, ins, piece).astype(out_ref.dtype)


def total(terms, cuts):
    layout, kept = narrow(terms, cuts[0][0], cuts[-1][1])
    part, width = kept[0].shape[-2:]
    return call(
        functools.partial(total_kernel, layout, cuts),
        kept,
        [VMEM] * len(kept),
        [jax.ShapeDtypeStruct((high - low, part, width), kept[0].dtype) for low, high in cuts],
        name="total",
    )


def finish_kernel(layouts, hidden_ref, *refs):
    out_ref, at = refs[-1], 0
    for batch, layout in enumerate(layouts):
        mixed = sum_of(layout, refs[at:-1], 0)
        out_ref[batch] = (hidden_ref[batch].astype(jnp.float32) + mixed).astype(out_ref.dtype)
        at += sum(count for _, _, count in layout)


def finish(hidden_in, terms):
    layouts, arrays = [], []
    for batch in terms:
        layout, kept = narrow(batch, 0, 1)
        layouts.append(layout)
        arrays += kept
    return call(
        functools.partial(finish_kernel, layouts),
        [hidden_in, *arrays],
        [VMEM] * (1 + len(arrays)),
        [jax.ShapeDtypeStruct(hidden_in.shape, hidden_in.dtype)],
        name="finish",
        pin=False,
    )[0]


def local(
    hidden_in,
    expert_ids,
    route_share,
    norm_gain,
    gate_weight,
    up_weight,
    down_weight,
    exponent_table,
):
    owners = lax.axis_size("ep")
    batches = hidden_in.shape[0]
    table = exponent_table.transpose(1, 0, 2)

    line = owners // 4
    half = line // 2

    def along_line(rows, place_of):
        return lax.ppermute(rows, "ep", [(i, place_of(i // 4) * 4 + i % 4) for i in range(owners)])

    def mirrored(p, span):
        return p // span * span + span - 1 - p % span

    def mirror(rows, span):
        return along_line(rows, lambda p: mirrored(p, span))

    def to_mid(rows):
        return lax.ppermute(rows, "ep", [(i, i ^ 2) for i in range(owners)])

    def to_core(rows):
        return lax.ppermute(rows, "ep", [(i, i ^ 1) for i in range(owners)])

    spans = []
    while line >> len(spans) > 2:
        spans.append(line >> len(spans))

    def owner_of(p, piece):
        if piece >= half:
            p, piece = mirrored(p, 2), piece - half
        for level in range(len(spans), 0, -1):
            if piece >= 1 << (level - 1):
                p, piece = mirrored(p, spans[level - 1]), piece - (1 << (level - 1))
        return p

    payload = prepare(hidden_in, expert_ids, route_share, norm_gain, -(-owners // LANES) * LANES)

    weights = load([gate_weight, up_weight, down_weight])
    there = [[to_mid(rows)] for rows in payload]
    near, far, joined = [], [], []
    for batch, rows in enumerate(payload):
        if batch:
            rows = after(rows, joined[-1])
        near.append([rows])
        for span in spans:
            received = mirror(rows, span)
            received = after(received, *([far[-1]] if batch else [*weights, *[x for xs in there for x in xs]]))
            near[batch].append(received)
            rows = join([rows, received])
            if not batch:
                there[batch].append(to_mid(received))
        joined.append(rows)
        far.append(mirror(rows if not batch else after(rows, *there[0]), 2))
    for batch in range(batches):
        there[batch].append(to_mid(join([*near[batch][1:], far[batch]]) if batch else far[batch]))

    def swap(arrays):
        return [to_core(x) for x in arrays]

    def sums(calls, slot):
        other = []
        for _, shares in calls:
            count = len(shares) // 2
            other += shares[slot * count : (slot + 1) * count]
        return [(slot, [mine for mine, _ in calls]), (None, other)]

    early = [[*near[batch], far[batch], *there[batch][:-1]] for batch in range(batches)]
    early_core = [swap(xs) if batch else None for batch, xs in enumerate(early)]
    terms, sent, back = [], [], []
    for batch in range(batches):
        order = [x for xs in early_core[batch + 1 : batch + 2] for x in xs]
        calls = []
        if batch == 0:
            xs = [*near[0], *there[0][:-1]]
            mine, *other = ffn([after(xs[0], *joined[1:2]), *xs[1:], *swap(xs)], table, weights)
            calls.append((mine, swap(other)))
            xs = [far[0], after(there[0][-1], mine)]
            xs += swap(xs)
            order += calls[0][1]
        else:
            late = after(there[batch][-1], sent[-1])
            xs = [*early[batch], late, *early_core[batch], to_core(late)]
            order += calls_before[-1][1][: SHARES // 2]
        mine, *other = ffn([after(xs[0], *order), *xs[1:]], table, weights)
        calls.append((mine, swap(other)))
        calls_before = calls
        out = sums(calls, 1)
        if batch + 1 < batches:
            sent += total(out, [(0, line)])
            back.append([to_mid(sent[-1])])
        else:
            sent += total(out, [(half, line)])
            back.append([to_mid(total(out, [(0, half)])[0]), to_mid(sent[-1])])
        terms.append([*sums(calls, 0), (None, back[-1])])

    for batch in range(batches):
        mixed = terms[batch]
        if batch + 1 < batches:
            mixed[-1] = (None, [after(back[batch][0], sent[-1])])
            mixed.append((None, [mirror(total(mixed, [(half, line)])[0], 2)]))
            span, pieces = 4, half
            while pieces > 1:
                part = total(mixed, [(pieces // 2, pieces)])[0]
                mixed.append((None, [mirror(part, span)]))
                span, pieces = span * 2, pieces // 2
        else:
            far_parts = total(mixed, [(j, j + 1) for j in range(half, line)])
            mixed[-1] = (None, [after(mixed[-1][1][0], *far_parts, part), *mixed[-1][1][1:]])
            parts = total(mixed, [(j, j + 1) for j in range(1, half)]) + far_parts
            mixed += [
                (None, [along_line(part, lambda p, j=j: owner_of(p, j))]) for j, part in enumerate(parts, 1)
            ]
    return finish(hidden_in, terms)


def solution(mesh):
    return jax.shard_map(
        local,
        mesh=mesh,
        in_specs=(
            P(None, ("grp", "ep"), None),
            P(None, ("grp", "ep"), None),
            P(None, ("grp", "ep"), None),
            P(),
            P("ep", None, None),
            P("ep", None, None),
            P("ep", None, None),
            P("ep", None, None),
        ),
        out_specs=P(None, ("grp", "ep"), None),
        check_vma=False,
    )
```

```python
import functools

import jax
import jax.numpy as jnp
from jax import lax
from jax.experimental import pallas as pl
from jax.experimental.pallas import tpu as pltpu
from jax.sharding import PartitionSpec as P

LANES = 128
SHARES = 4
VMEM = pl.BlockSpec(memory_space=pltpu.VMEM)
HBM = pl.BlockSpec(memory_space=pltpu.HBM)
SMEM = pl.BlockSpec(memory_space=pltpu.SMEM)
PINNED = {pltpu.VMEM, pltpu.HBM}


def call(kernel, operands, specs, shapes, scratch=(), name=None, vmem=8, pin=True):
    if pin:
        shapes = [pltpu.VMEM(s.shape, s.dtype) for s in shapes]
        operands = [
            pltpu.with_memory_space_constraint(a, spec.memory_space)
            if spec.memory_space in PINNED
            else a
            for a, spec in zip(operands, specs)
        ]
    return pl.pallas_call(
        kernel,
        out_shape=shapes,
        in_specs=specs,
        out_specs=[VMEM] * len(shapes),
        scratch_shapes=list(scratch),
        cost_estimate=pl.CostEstimate(flops=0, bytes_accessed=0, transcendentals=0),
        compiler_params=pltpu.CompilerParams(vmem_limit_bytes=vmem << 20),
        name=name,
    )(*operands)


def after(value, *others):
    return lax.optimization_barrier((value, *others))[0]


def prepare_kernel(hidden_hbm, ids_hbm, share_hbm, gain_hbm, *refs):
    out_refs, (hidden_ref, ids_ref, share_ref, gain_ref, sems) = refs[:-5], refs[-5:]
    sources = (hidden_hbm, ids_hbm, share_hbm, gain_hbm)
    targets = (hidden_ref, ids_ref, share_ref, gain_ref)
    copies = [pltpu.make_async_copy(s, t, sems.at[i]) for i, (s, t) in enumerate(zip(sources, targets))]
    for copy in copies:
        copy.start()
    for copy in copies:
        copy.wait()
    rows, width = hidden_ref.shape[1:]
    fanout = ids_ref.shape[1]
    extra = out_refs[0].shape[2] - width
    for batch, out_ref in enumerate(out_refs):
        values = hidden_ref[batch].astype(jnp.float32)
        power = jnp.mean(values * values, axis=-1, keepdims=True)
        normed = values * lax.rsqrt(power + 1e-06) * gain_ref[...]
        out_ref[0, :, :width] = normed.astype(jnp.bfloat16)
        expert = lax.broadcasted_iota(jnp.int32, (extra, rows), 0)
        dense = jnp.zeros((extra, rows), jnp.float32)
        for k in range(fanout):
            share = share_ref[batch, k : k + 1, :].astype(jnp.float32) * (1.0 / 64.0)
            dense = dense + jnp.where(expert == ids_ref[batch, k : k + 1, :], share, 0.0)
        out_ref[0, :, width:] = dense.T.astype(jnp.bfloat16)


def prepare(hidden_in, expert_ids, route_share, norm_gain, extra):
    batches, rows, width = hidden_in.shape
    operands = [
        hidden_in,
        expert_ids.transpose(0, 2, 1),
        route_share.transpose(0, 2, 1),
        norm_gain.reshape(1, width),
    ]
    return call(
        prepare_kernel,
        operands,
        [HBM] * 4,
        [jax.ShapeDtypeStruct((1, rows, width + extra), jnp.bfloat16)] * batches,
        [pltpu.VMEM(a.shape, a.dtype) for a in operands] + [pltpu.SemaphoreType.DMA((4,))],
        name="prepare",
    )


def join_kernel(*refs):
    at = 0
    for ref in refs[:-1]:
        refs[-1][at : at + ref.shape[0]] = ref[...]
        at += ref.shape[0]


def join(pieces):
    shape = (sum(p.shape[0] for p in pieces), *pieces[0].shape[1:])
    shape = jax.ShapeDtypeStruct(shape, pieces[0].dtype)
    return call(join_kernel, pieces, [VMEM] * len(pieces), [shape], name="join")[0]


def load_kernel(*refs):
    count = len(refs) // 2
    copies = [pltpu.make_async_copy(refs[i], refs[count + i], refs[-1].at[i]) for i in range(count)]
    for copy in copies:
        copy.start()
    for copy in copies:
        copy.wait()


def load(weights):
    return call(
        load_kernel,
        weights,
        [HBM] * len(weights),
        [jax.ShapeDtypeStruct(w.shape, w.dtype) for w in weights],
        [pltpu.SemaphoreType.DMA((len(weights),))],
        name="load",
    )


def ffn_kernel(table_ref, gate_ref, up_ref, down_ref, *refs):
    x_refs, outs, (x_all, hidden) = refs[: -3 - SHARES], refs[-3 - SHARES : -2], refs[-2:]
    mine_ref, other_refs = outs[0], outs[1:]
    width, ff = gate_ref.shape[1:]
    group = ff // table_ref.shape[2]
    step = 2 * group if ff % (2 * group) == 0 else group
    _, pieces, part, _ = mine_ref.shape
    at = 0
    for x_ref in x_refs:
        rows = x_ref.shape[0] * part
        x_all[at : at + rows, :] = x_ref[...].reshape(rows, x_ref.shape[2])
        at += rows

    def scale(which, b):
        return jnp.exp2(jnp.full((1, group), table_ref[which, 0, b], jnp.int32).astype(jnp.float32))

    for f in range(0, ff, step):
        x = x_all[:, :width]
        gate = jnp.dot(x, gate_ref[0, :, f : f + step], preferred_element_type=jnp.float32)
        up = jnp.dot(x, up_ref[0, :, f : f + step], preferred_element_type=jnp.float32)
        for at in range(0, step, group):
            b = (f + at) // group
            g = gate[:, at : at + group] * scale(0, b)
            u = up[:, at : at + group] * scale(1, b)
            h = g / (1.0 + jnp.exp(-g)) * u * scale(2, b)
            hidden[:, f + at : f + at + group] = h.astype(jnp.bfloat16)
    shares = x_all[:, width:].astype(jnp.float32)
    here = lax.broadcasted_iota(jnp.int32, shares.shape, 1) == lax.axis_index("ep")
    weight = jnp.sum(jnp.where(here, shares, 0.0), axis=1, keepdims=True)
    cols = 512 if width % 512 == 0 else LANES
    for n in range(0, width, cols):
        out = jnp.dot(hidden[...], down_ref[0, :, n : n + cols], preferred_element_type=jnp.float32)
        out = (out * weight).astype(jnp.bfloat16).reshape(4, pieces, part, cols)
        mine_ref[:, :, :, n : n + cols] = out[:2]
        other = out[2:].reshape(2 * pieces, part, cols)
        for i, other_ref in enumerate(other_refs):
            at = i * other_ref.shape[0]
            other_ref[:, :, n : n + cols] = other[at : at + other_ref.shape[0]]


def ffn(xs, table, weights):
    pieces = sum(x.shape[0] for x in xs) // 4
    _, part, full = xs[0].shape
    width, ff = weights[0].shape[1:]
    rows = 4 * pieces * part
    return call(
        ffn_kernel,
        [table, *weights, *xs],
        [SMEM] + [VMEM] * (3 + len(xs)),
        [jax.ShapeDtypeStruct((2, pieces, part, width), jnp.bfloat16)]
        + [jax.ShapeDtypeStruct((2 * pieces // SHARES, part, width), jnp.bfloat16)] * SHARES,
        [pltpu.VMEM((rows, full), jnp.bfloat16), pltpu.VMEM((rows, ff), jnp.bfloat16)],
        name="ffn",
        vmem=16,
    )


def pieces_in(slot, array):
    return array.shape[0 if slot is None else 1]


def sum_of(layout, refs, piece):
    result, at = None, 0
    for slot, skip, count in layout:
        i = piece - skip
        for ref in refs[at : at + count]:
            if 0 <= i < pieces_in(slot, ref):
                term = (ref[i] if slot is None else ref[slot, i]).astype(jnp.float32)
                result = term if result is None else result + term
            i -= pieces_in(slot, ref)
        at += count
    return result


def narrow(terms, low, high):
    layout, kept = [], []
    for slot, arrays in terms:
        skip = 0
        while low >= skip + pieces_in(slot, arrays[0]):
            skip, arrays = skip + pieces_in(slot, arrays[0]), arrays[1:]
        while high <= skip + sum(pieces_in(slot, a) for a in arrays[:-1]):
            arrays = arrays[:-1]
        layout.append((slot, skip, len(arrays)))
        kept += arrays
    return layout, kept


def total_kernel(layout, cuts, *refs):
    ins, outs = refs[: -len(cuts)], refs[-len(cuts) :]
    for (low, high), out_ref in zip(cuts, outs):
        for piece in range(low, high):
            out_ref[piece - low] = sum_of(layout, ins, piece).astype(out_ref.dtype)


def total(terms, cuts):
    layout, kept = narrow(terms, cuts[0][0], cuts[-1][1])
    part, width = kept[0].shape[-2:]
    return call(
        functools.partial(total_kernel, layout, cuts),
        kept,
        [VMEM] * len(kept),
        [jax.ShapeDtypeStruct((high - low, part, width), kept[0].dtype) for low, high in cuts],
        name="total",
    )


def finish_kernel(layouts, hidden_ref, *refs):
    out_ref, at = refs[-1], 0
    for batch, layout in enumerate(layouts):
        mixed = sum_of(layout, refs[at:-1], 0)
        out_ref[batch] = (hidden_ref[batch].astype(jnp.float32) + mixed).astype(out_ref.dtype)
        at += sum(count for _, _, count in layout)


def finish(hidden_in, terms):
    layouts, arrays = [], []
    for batch in terms:
        layout, kept = narrow(batch, 0, 1)
        layouts.append(layout)
        arrays += kept
    return call(
        functools.partial(finish_kernel, layouts),
        [hidden_in, *arrays],
        [VMEM] * (1 + len(arrays)),
        [jax.ShapeDtypeStruct(hidden_in.shape, hidden_in.dtype)],
        name="finish",
        pin=False,
    )[0]


def local(
    hidden_in,
    expert_ids,
    route_share,
    norm_gain,
    gate_weight,
    up_weight,
    down_weight,
    exponent_table,
):
    owners = lax.axis_size("ep")
    batches = hidden_in.shape[0]
    table = exponent_table.transpose(1, 0, 2)

    line = owners // 4
    half = line // 2

    def along_line(rows, place_of):
        return lax.ppermute(rows, "ep", [(i, place_of(i // 4) * 4 + i % 4) for i in range(owners)])

    def mirrored(p, span):
        return p // span * span + span - 1 - p % span

    def mirror(rows, span):
        return along_line(rows, lambda p: mirrored(p, span))

    def to_mid(rows):
        return lax.ppermute(rows, "ep", [(i, i ^ 2) for i in range(owners)])

    def to_core(rows):
        return lax.ppermute(rows, "ep", [(i, i ^ 1) for i in range(owners)])

    spans = []
    while line >> len(spans) > 2:
        spans.append(line >> len(spans))

    payload = prepare(hidden_in, expert_ids, route_share, norm_gain, -(-owners // LANES) * LANES)

    weights = load([gate_weight, up_weight, down_weight])
    there = [[to_mid(rows)] for rows in payload]
    near, far, joined = [], [], []
    for batch, rows in enumerate(payload):
        if batch:
            rows = after(rows, joined[-1])
        near.append([rows])
        for span in spans:
            received = mirror(rows, span)
            received = after(received, *([far[-1]] if batch else [*weights, *[x for xs in there for x in xs]]))
            near[batch].append(received)
            rows = join([rows, received])
            if not batch:
                there[batch].append(to_mid(received))
        joined.append(rows)
        far.append(mirror(rows if not batch else after(rows, *there[0]), 2))
    for batch in range(batches):
        there[batch].append(to_mid(join([*near[batch][1:], far[batch]]) if batch else far[batch]))

    def swap(arrays):
        return [to_core(x) for x in arrays]

    def sums(calls, slot):
        other = []
        for _, shares in calls:
            count = len(shares) // 2
            other += shares[slot * count : (slot + 1) * count]
        return [(slot, [mine for mine, _ in calls]), (None, other)]

    early = [[*near[batch], far[batch], *there[batch][:-1]] for batch in range(batches)]
    early_core = [swap(xs) if batch else None for batch, xs in enumerate(early)]
    terms, sent, back = [], [], []
    for batch in range(batches):
        order = [x for xs in early_core[batch + 1 : batch + 2] for x in xs]
        calls = []
        if batch == 0:
            xs = [*near[0], *there[0][:-1]]
            mine, *other = ffn([after(xs[0], *joined[1:2]), *xs[1:], *swap(xs)], table, weights)
            calls.append((mine, swap(other)))
            xs = [far[0], after(there[0][-1], mine)]
            xs += swap(xs)
            order += calls[0][1]
        else:
            late = after(there[batch][-1], sent[-1])
            xs = [*early[batch], late, *early_core[batch], to_core(late)]
            order += calls_before[-1][1][: SHARES // 2]
        mine, *other = ffn([after(xs[0], *order), *xs[1:]], table, weights)
        calls.append((mine, swap(other)))
        calls_before = calls
        out = sums(calls, 1)
        if batch + 1 < batches:
            sent += total(out, [(0, line)])
            back.append([to_mid(sent[-1])])
        else:
            sent += total(out, [(half, line)])
            back.append([to_mid(total(out, [(0, half)])[0]), to_mid(sent[-1])])
        terms.append([*sums(calls, 0), (None, back[-1])])

    for batch in range(batches):
        mixed = terms[batch]
        if batch + 1 < batches:
            mixed[-1] = (None, [after(back[batch][0], sent[-1])])
        mixed.append((None, [mirror(total(mixed, [(half, line)])[0], 2)]))
        span, pieces = 4, half
        while pieces > 1:
            mixed.append((None, [mirror(total(mixed, [(pieces // 2, pieces)])[0], span)]))
            span, pieces = span * 2, pieces // 2
    return finish(hidden_in, terms)


def solution(mesh):
    return jax.shard_map(
        local,
        mesh=mesh,
        in_specs=(
            P(None, ("grp", "ep"), None),
            P(None, ("grp", "ep"), None),
            P(None, ("grp", "ep"), None),
            P(),
            P("ep", None, None),
            P("ep", None, None),
            P("ep", None, None),
            P("ep", None, None),
        ),
        out_specs=P(None, ("grp", "ep"), None),
        check_vma=False,
    )
```

```python
import functools

import jax
import jax.numpy as jnp
from jax import lax
from jax.experimental import pallas as pl
from jax.experimental.pallas import tpu as pltpu
from jax.sharding import PartitionSpec as P

LANES = 128
SHARES = 4
VMEM = pl.BlockSpec(memory_space=pltpu.VMEM)
HBM = pl.BlockSpec(memory_space=pltpu.HBM)
SMEM = pl.BlockSpec(memory_space=pltpu.SMEM)
PINNED = {pltpu.VMEM, pltpu.HBM}


def call(kernel, operands, specs, shapes, scratch=(), name=None, vmem=8, pin=True):
    if pin:
        shapes = [pltpu.VMEM(s.shape, s.dtype) for s in shapes]
        operands = [
            pltpu.with_memory_space_constraint(a, spec.memory_space)
            if spec.memory_space in PINNED
            else a
            for a, spec in zip(operands, specs)
        ]
    return pl.pallas_call(
        kernel,
        out_shape=shapes,
        in_specs=specs,
        out_specs=[VMEM] * len(shapes),
        scratch_shapes=list(scratch),
        cost_estimate=pl.CostEstimate(flops=0, bytes_accessed=0, transcendentals=0),
        compiler_params=pltpu.CompilerParams(vmem_limit_bytes=vmem << 20),
        name=name,
    )(*operands)


def after(value, *others):
    return lax.optimization_barrier((value, *others))[0]


def prepare_kernel(hidden_hbm, ids_hbm, share_hbm, gain_hbm, *refs):
    out_refs, (hidden_ref, ids_ref, share_ref, gain_ref, sems) = refs[:-5], refs[-5:]
    sources = (hidden_hbm, ids_hbm, share_hbm, gain_hbm)
    targets = (hidden_ref, ids_ref, share_ref, gain_ref)
    copies = [pltpu.make_async_copy(s, t, sems.at[i]) for i, (s, t) in enumerate(zip(sources, targets))]
    for copy in copies:
        copy.start()
    for copy in copies:
        copy.wait()
    rows, width = hidden_ref.shape[1:]
    fanout = ids_ref.shape[1]
    extra = out_refs[0].shape[2] - width
    for batch, out_ref in enumerate(out_refs):
        values = hidden_ref[batch].astype(jnp.float32)
        power = jnp.mean(values * values, axis=-1, keepdims=True)
        normed = values * lax.rsqrt(power + 1e-06) * gain_ref[...]
        out_ref[0, :, :width] = normed.astype(jnp.bfloat16)
        expert = lax.broadcasted_iota(jnp.int32, (extra, rows), 0)
        dense = jnp.zeros((extra, rows), jnp.float32)
        for k in range(fanout):
            share = share_ref[batch, k : k + 1, :].astype(jnp.float32) * (1.0 / 64.0)
            dense = dense + jnp.where(expert == ids_ref[batch, k : k + 1, :], share, 0.0)
        out_ref[0, :, width:] = dense.T.astype(jnp.bfloat16)


def prepare(hidden_in, expert_ids, route_share, norm_gain, extra):
    batches, rows, width = hidden_in.shape
    operands = [
        hidden_in,
        expert_ids.transpose(0, 2, 1),
        route_share.transpose(0, 2, 1),
        norm_gain.reshape(1, width),
    ]
    return call(
        prepare_kernel,
        operands,
        [HBM] * 4,
        [jax.ShapeDtypeStruct((1, rows, width + extra), jnp.bfloat16)] * batches,
        [pltpu.VMEM(a.shape, a.dtype) for a in operands] + [pltpu.SemaphoreType.DMA((4,))],
        name="prepare",
    )


def join_kernel(*refs):
    at = 0
    for ref in refs[:-1]:
        refs[-1][at : at + ref.shape[0]] = ref[...]
        at += ref.shape[0]


def join(pieces):
    shape = (sum(p.shape[0] for p in pieces), *pieces[0].shape[1:])
    shape = jax.ShapeDtypeStruct(shape, pieces[0].dtype)
    return call(join_kernel, pieces, [VMEM] * len(pieces), [shape], name="join")[0]


def load_kernel(*refs):
    count = len(refs) // 2
    copies = [pltpu.make_async_copy(refs[i], refs[count + i], refs[-1].at[i]) for i in range(count)]
    for copy in copies:
        copy.start()
    for copy in copies:
        copy.wait()


def load(weights):
    return call(
        load_kernel,
        weights,
        [HBM] * len(weights),
        [jax.ShapeDtypeStruct(w.shape, w.dtype) for w in weights],
        [pltpu.SemaphoreType.DMA((len(weights),))],
        name="load",
    )


def ffn_kernel(table_ref, gate_ref, up_ref, down_ref, *refs):
    x_refs, outs, (x_all, hidden) = refs[: -3 - SHARES], refs[-3 - SHARES : -2], refs[-2:]
    mine_ref, other_refs = outs[0], outs[1:]
    width, ff = gate_ref.shape[1:]
    group = ff // table_ref.shape[2]
    step = 2 * group if ff % (2 * group) == 0 else group
    _, pieces, part, _ = mine_ref.shape
    at = 0
    for x_ref in x_refs:
        rows = x_ref.shape[0] * part
        x_all[at : at + rows, :] = x_ref[...].reshape(rows, x_ref.shape[2])
        at += rows

    def scale(which, b):
        return jnp.exp2(jnp.full((1, group), table_ref[which, 0, b], jnp.int32).astype(jnp.float32))

    for f in range(0, ff, step):
        x = x_all[:, :width]
        gate = jnp.dot(x, gate_ref[0, :, f : f + step], preferred_element_type=jnp.float32)
        up = jnp.dot(x, up_ref[0, :, f : f + step], preferred_element_type=jnp.float32)
        for at in range(0, step, group):
            b = (f + at) // group
            g = gate[:, at : at + group] * scale(0, b)
            u = up[:, at : at + group] * scale(1, b)
            h = g / (1.0 + jnp.exp(-g)) * u * scale(2, b)
            hidden[:, f + at : f + at + group] = h.astype(jnp.bfloat16)
    shares = x_all[:, width:].astype(jnp.float32)
    here = lax.broadcasted_iota(jnp.int32, shares.shape, 1) == lax.axis_index("ep")
    weight = jnp.sum(jnp.where(here, shares, 0.0), axis=1, keepdims=True)
    cols = 512 if width % 512 == 0 else LANES
    for n in range(0, width, cols):
        out = jnp.dot(hidden[...], down_ref[0, :, n : n + cols], preferred_element_type=jnp.float32)
        out = (out * weight).astype(jnp.bfloat16).reshape(4, pieces, part, cols)
        mine_ref[:, :, :, n : n + cols] = out[:2]
        other = out[2:].reshape(2 * pieces, part, cols)
        for i, other_ref in enumerate(other_refs):
            at = i * other_ref.shape[0]
            other_ref[:, :, n : n + cols] = other[at : at + other_ref.shape[0]]


def ffn(xs, table, weights):
    pieces = sum(x.shape[0] for x in xs) // 4
    _, part, full = xs[0].shape
    width, ff = weights[0].shape[1:]
    rows = 4 * pieces * part
    return call(
        ffn_kernel,
        [table, *weights, *xs],
        [SMEM] + [VMEM] * (3 + len(xs)),
        [jax.ShapeDtypeStruct((2, pieces, part, width), jnp.bfloat16)]
        + [jax.ShapeDtypeStruct((2 * pieces // SHARES, part, width), jnp.bfloat16)] * SHARES,
        [pltpu.VMEM((rows, full), jnp.bfloat16), pltpu.VMEM((rows, ff), jnp.bfloat16)],
        name="ffn",
        vmem=16,
    )


def pieces_in(slot, array):
    return array.shape[0 if slot is None else 1]


def sum_of(layout, refs, piece):
    result, at = None, 0
    for slot, skip, count in layout:
        i = piece - skip
        for ref in refs[at : at + count]:
            if 0 <= i < pieces_in(slot, ref):
                term = (ref[i] if slot is None else ref[slot, i]).astype(jnp.float32)
                result = term if result is None else result + term
            i -= pieces_in(slot, ref)
        at += count
    return result


def narrow(terms, low, high):
    layout, kept = [], []
    for slot, arrays in terms:
        skip = 0
        while low >= skip + pieces_in(slot, arrays[0]):
            skip, arrays = skip + pieces_in(slot, arrays[0]), arrays[1:]
        while high <= skip + sum(pieces_in(slot, a) for a in arrays[:-1]):
            arrays = arrays[:-1]
        layout.append((slot, skip, len(arrays)))
        kept += arrays
    return layout, kept


def total_kernel(layout, cuts, *refs):
    ins, outs = refs[: -len(cuts)], refs[-len(cuts) :]
    for (low, high), out_ref in zip(cuts, outs):
        for piece in range(low, high):
            out_ref[piece - low] = sum_of(layout, ins, piece).astype(out_ref.dtype)


def total(terms, cuts):
    layout, kept = narrow(terms, cuts[0][0], cuts[-1][1])
    part, width = kept[0].shape[-2:]
    return call(
        functools.partial(total_kernel, layout, cuts),
        kept,
        [VMEM] * len(kept),
        [jax.ShapeDtypeStruct((high - low, part, width), kept[0].dtype) for low, high in cuts],
        name="total",
    )


def finish_kernel(layouts, hidden_ref, *refs):
    out_ref, at = refs[-1], 0
    for batch, layout in enumerate(layouts):
        mixed = sum_of(layout, refs[at:-1], 0)
        out_ref[batch] = (hidden_ref[batch].astype(jnp.float32) + mixed).astype(out_ref.dtype)
        at += sum(count for _, _, count in layout)


def finish(hidden_in, terms):
    layouts, arrays = [], []
    for batch in terms:
        layout, kept = narrow(batch, 0, 1)
        layouts.append(layout)
        arrays += kept
    return call(
        functools.partial(finish_kernel, layouts),
        [hidden_in, *arrays],
        [VMEM] * (1 + len(arrays)),
        [jax.ShapeDtypeStruct(hidden_in.shape, hidden_in.dtype)],
        name="finish",
        pin=False,
    )[0]


def local(
    hidden_in,
    expert_ids,
    route_share,
    norm_gain,
    gate_weight,
    up_weight,
    down_weight,
    exponent_table,
):
    owners = lax.axis_size("ep")
    batches = hidden_in.shape[0]
    table = exponent_table.transpose(1, 0, 2)

    line = owners // 4
    half = line // 2

    def along_line(rows, place_of):
        return lax.ppermute(rows, "ep", [(i, place_of(i // 4) * 4 + i % 4) for i in range(owners)])

    def mirrored(p, span):
        return p // span * span + span - 1 - p % span

    def mirror(rows, span):
        return along_line(rows, lambda p: mirrored(p, span))

    def to_mid(rows):
        return lax.ppermute(rows, "ep", [(i, i ^ 2) for i in range(owners)])

    def to_core(rows):
        return lax.ppermute(rows, "ep", [(i, i ^ 1) for i in range(owners)])

    spans = []
    while line >> len(spans) > 2:
        spans.append(line >> len(spans))

    payload = prepare(hidden_in, expert_ids, route_share, norm_gain, -(-owners // LANES) * LANES)

    weights = load([gate_weight, up_weight, down_weight])
    there = [[to_mid(rows)] for rows in payload]
    near, far, joined = [], [], []
    for batch, rows in enumerate(payload):
        if batch:
            rows = after(rows, joined[-1])
        near.append([rows])
        for span in spans:
            received = mirror(rows, span)
            received = after(received, *([far[-1]] if batch else [*weights, *[x for xs in there for x in xs]]))
            near[batch].append(received)
            rows = join([rows, received])
            if not batch:
                there[batch].append(to_mid(received))
        joined.append(rows)
        far.append(mirror(rows if not batch else after(rows, *there[0]), 2))
    for batch in range(batches):
        there[batch].append(to_mid(join([*near[batch][1:], far[batch]]) if batch else far[batch]))

    def swap(arrays):
        return [to_core(x) for x in arrays]

    def sums(calls, slot):
        other = []
        for _, shares in calls:
            count = len(shares) // 2
            other += shares[slot * count : (slot + 1) * count]
        return [(slot, [mine for mine, _ in calls]), (None, other)]

    early = [[*near[batch], far[batch], *there[batch][:-1]] for batch in range(batches)]
    early_core = [swap(xs) if batch else None for batch, xs in enumerate(early)]
    terms, sent, back = [], [], []
    for batch in range(batches):
        order = [x for xs in early_core[batch + 1 : batch + 2] for x in xs]
        calls = []
        if batch == 0:
            xs = [*near[0], *there[0][:-1]]
            mine, *other = ffn([after(xs[0], *joined[1:2]), *xs[1:], *swap(xs)], table, weights)
            calls.append((mine, swap(other)))
            xs = [far[0], after(there[0][-1], mine)]
            xs += swap(xs)
            order += calls[0][1]
        else:
            late = after(there[batch][-1], sent[-1], *calls_before[-1][1][: SHARES // 2])
            xs = [*early[batch], late, *early_core[batch], to_core(late)]
            order += calls_before[-1][1][: SHARES // 2]
        mine, *other = ffn([after(xs[0], *order), *xs[1:]], table, weights)
        calls.append((mine, swap(other)))
        calls_before = calls
        out = sums(calls, 1)
        if batch + 1 < batches:
            sent += total(out, [(0, line)])
            back.append([to_mid(sent[-1])])
        else:
            sent += total(out, [(half, line)])
            back.append([to_mid(total(out, [(0, half)])[0]), to_mid(sent[-1])])
        terms.append([*sums(calls, 0), (None, back[-1])])

    for batch in range(batches):
        mixed = terms[batch]
        if batch + 1 < batches:
            mixed[-1] = (None, [after(back[batch][0], sent[-1])])
        mixed.append((None, [mirror(total(mixed, [(half, line)])[0], 2)]))
        span, pieces = 4, half
        while pieces > 1:
            mixed.append((None, [mirror(total(mixed, [(pieces // 2, pieces)])[0], span)]))
            span, pieces = span * 2, pieces // 2
    return finish(hidden_in, terms)


def solution(mesh):
    return jax.shard_map(
        local,
        mesh=mesh,
        in_specs=(
            P(None, ("grp", "ep"), None),
            P(None, ("grp", "ep"), None),
            P(None, ("grp", "ep"), None),
            P(),
            P("ep", None, None),
            P("ep", None, None),
            P("ep", None, None),
            P("ep", None, None),
        ),
        out_specs=P(None, ("grp", "ep"), None),
        check_vma=False,
    )
```
